32 devices in a mesh: row: 8 (over z, x), col: 4 (over y, core).
Axes of the slice: x: 2, y: 2, z: 4, core: 2. Of those that a mesh axis runs over, the one named last changes fastest.
Arguments:
- data: float32 [32768, 4096], P('row', 'col'), may hold values from -17 to 17
- omega: float32 [4096, 128], P('col'), may hold values from -0.09375 to 0.09375
Outputs:
- basis: float32 [32768, 128], P(('row', 'col'))
- projected: float32 [128, 4096], P(None, 'col')
- small_gram: float32 [128, 128], replicated
The draws below stay inside these ranges and needn't reach their ends.
All inputs are finite; a program needn't handle non-finite values.
Results may differ from the reference program's by a relative error of at most 0.0003.
Values sent between devices are 32-bit elements; how exact they have to be, the bound alone decides.
No kernel may reach another device: no remote copies, remote signals or barrier semaphores. Data moves between devices by JAX's collectives and lax.ppermute only.
A program may use at most 64 MiB of HBM per device.

```python
import jax
import jax.numpy as jnp
from jax import lax

COLS = 4096
SKETCH = 128
ROWS = 32768


def draw_data(key, part):
    key = jax.random.fold_in(key, 11)
    first, second = jax.random.split(key, 2)
    colscale = jnp.exp(jax.random.uniform(second, (1, COLS), jnp.float32) * jnp.log(10.0))
    base = jnp.clip(jax.random.normal(first, (ROWS, COLS), jnp.float32), -5.0, 5.0)
    values = base * colscale / 3.0
    return values.astype(jnp.float32)


def levels(stream_key, dims, cuts, least, top_value):
    gain, own = 1.0, jax.random.fold_in(stream_key, 6)
    for axis_at, shards_of in cuts:
        steps = jnp.exp(jax.random.uniform(jax.random.fold_in(own, axis_at), (shards_of,), jnp.float32, least / len(cuts), top_value / len(cuts)))
        gain = gain * jnp.repeat(steps, dims[axis_at] // shards_of).reshape([-1 if axis == axis_at else 1 for axis in range(len(dims))])
    return gain


def bell_draw(own_key, shape, width, bound, cuts=(), kind=jnp.bfloat16):
    result = width * jax.random.normal(own_key, shape, jnp.float32)
    if cuts:
        result = result * levels(own_key, shape, cuts, -0.22, 0.18)
    return jnp.clip(result, -bound, bound).astype(kind)


def setup_inputs(seed: int = 0) -> dict:
    arg_keys = jax.random.split(jax.random.key(seed), 3)
    return {
        "data": draw_data(jax.random.fold_in(arg_keys[2], 71), 0),
        "omega": bell_draw(arg_keys[1], (COLS, SKETCH), COLS ** -0.5, 0.09375, ((0, 4),), jnp.float32),
    }


def reference(data, omega):
    high = lax.Precision.HIGHEST
    sketch = jnp.dot(data.astype(jnp.float32), omega.astype(jnp.float32), precision=high, preferred_element_type=jnp.float32)
    basis, factor = jnp.linalg.qr(sketch)
    signs = jnp.sign(jnp.diagonal(factor))
    basis = basis * signs[None, :]
    projected = jnp.dot(basis.T.astype(jnp.float32), data.astype(jnp.float32), precision=high, preferred_element_type=jnp.float32)
    small_gram = jnp.dot(projected.astype(jnp.float32), projected.T.astype(jnp.float32), precision=high, preferred_element_type=jnp.float32) / ROWS
    return (basis, projected, small_gram)
```

```python
import functools

import jax
import jax.numpy as jnp
from jax import lax
from jax.experimental import pallas as pl
from jax.experimental.pallas import tpu as pltpu
from jax.sharding import PartitionSpec as P

high = lax.Precision.HIGHEST
f32 = jnp.float32
bf16 = jnp.bfloat16

BLOCK = 256
SLICE = 128
VMEM = 48 * 1024 * 1024


def split(value):
    upper = value.astype(bf16)
    return upper, (value - upper.astype(f32)).astype(bf16)


def swap(value, axis, bit):
    return lax.ppermute(value, axis, [(i, i ^ bit) for i in range(lax.axis_size(axis))])


def sketch_kernel(own_ref, data_ref, omega_ref, out_ref, wide_ref):
    @pl.when(pl.program_id(0) + pl.program_id(1) == 0)
    def _():
        upper, rest = split(omega_ref[...])
        width = omega_ref.shape[1]
        wide_ref[:, :width] = upper
        wide_ref[:, width:] = rest

    width = omega_ref.shape[1]
    upper, rest = split(data_ref[...])
    both = jnp.dot(upper, wide_ref[...], preferred_element_type=f32)
    more = jnp.dot(rest, wide_ref[:, :width], preferred_element_type=f32)
    out_ref[0] = both[:, :width] + both[:, width:] + more


def partial_sketch(own, data, omega, places, first, rows):
    quarter = data.shape[0] // lax.axis_size("col")
    per_quarter = quarter // BLOCK
    start = first // BLOCK
    steps = rows // BLOCK
    width = omega.shape[1]
    base = places[0]
    gap = places[1] - places[0]
    return pl.pallas_call(
        sketch_kernel,
        grid_spec=pltpu.PrefetchScalarGridSpec(
            num_scalar_prefetch=1,
            grid=(2, steps),
            in_specs=[
                pl.BlockSpec(
                    (BLOCK, data.shape[1]),
                    lambda p, i, own: (((base + gap * p) ^ own[0]) * per_quarter + start + i, 0),
                ),
                pl.BlockSpec(omega.shape, lambda p, i, own: (0, 0)),
            ],
            out_specs=pl.BlockSpec((1, BLOCK, width), lambda p, i, own: (p, i, 0)),
            scratch_shapes=[pltpu.VMEM((omega.shape[0], 2 * width), bf16)],
        ),
        out_shape=jax.ShapeDtypeStruct((2, rows, width), f32),
        compiler_params=pltpu.CompilerParams(vmem_limit_bytes=VMEM),
        cost_estimate=pl.CostEstimate(
            flops=2 * rows * data.shape[1] * width * 2 * 4,
            bytes_accessed=2 * rows * data.shape[1] * 4,
            transcendentals=0,
        ),
        name="partial_sketch",
    )(own, data, omega)


def project_kernel(count, split_out, own_ref, *refs):
    has_before = len(refs) > count + 1 + (3 if split_out else 1)
    data_ref = refs[0]
    parts = refs[1 : 1 + count]
    before = refs[1 + count] if has_before else None
    outs = refs[1 + count + (1 if has_before else 0) :]
    total = outs[-1] if split_out else outs[0]
    part, step = pl.program_id(0), pl.program_id(1)

    @pl.when(part + step == 0)
    def _():
        total[...] = before[...] if has_before else jnp.zeros_like(total)

    d_upper, d_rest = split(data_ref[...])
    for k in range(count):

        @pl.when(part == k)
        def _():
            turned = parts[k][...].T
            upper, rest = split(turned)
            both = jnp.dot(jnp.concatenate([upper, rest], 0), d_upper, preferred_element_type=f32)
            more = jnp.dot(upper, d_rest, preferred_element_type=f32)
            width = turned.shape[0]
            total[...] += both[:width] + both[width:] + more

    if split_out:
        send_ref, keep_ref = outs[0], outs[1]
        half = send_ref.shape[0]

        @pl.when((part == count - 1) & (step == pl.num_programs(1) - 1))
        def _():
            me = own_ref[1]
            for i in range(half):
                for ref, place in ((keep_ref, 2 * i), (send_ref, 2 * i + 1)):
                    at = pl.multiple_of((place ^ me) * SLICE, SLICE)
                    ref[i] = total[:, pl.ds(at, SLICE)]


def project(own, data, parts, places, first, before=None, split_out=False):
    count = len(parts)
    rows, width = parts[0].shape
    quarter = data.shape[0] // lax.axis_size("col")
    per_quarter = quarter // BLOCK
    start = first // BLOCK
    cols = data.shape[1]
    base = places[0]
    gap = places[1] - places[0] if count > 1 else 0
    whole = pl.BlockSpec((width, cols), lambda p, i, own: (0, 0))
    slices = cols // SLICE

    def part_spec(k):
        return pl.BlockSpec((BLOCK, width), lambda p, i, own: (jnp.where(p == k, i, 0 if k else rows // BLOCK - 1), 0))

    if split_out:
        half = pl.BlockSpec((slices // 2, width, SLICE), lambda p, i, own: (0, 0, 0))
        out_specs = [half, half]
        out_shape = [jax.ShapeDtypeStruct((slices // 2, width, SLICE), f32)] * 2
        scratch = [pltpu.VMEM((width, cols), f32)]
    else:
        out_specs = whole
        out_shape = jax.ShapeDtypeStruct((width, cols), f32)
        scratch = []
    args = [own, data, *parts]
    specs = [
        pl.BlockSpec(
            (BLOCK, cols),
            lambda p, i, own: (((base + gap * p) ^ own[0]) * per_quarter + start + i, 0),
        ),
        *[part_spec(k) for k in range(count)],
    ]
    if before is not None:
        args.append(before)
        specs.append(whole)
    return pl.pallas_call(
        functools.partial(project_kernel, count, split_out),
        grid_spec=pltpu.PrefetchScalarGridSpec(
            num_scalar_prefetch=1,
            grid=(count, rows // BLOCK),
            in_specs=specs,
            out_specs=out_specs,
            scratch_shapes=scratch,
        ),
        out_shape=out_shape,
        compiler_params=pltpu.CompilerParams(vmem_limit_bytes=VMEM),
        cost_estimate=pl.CostEstimate(
            flops=2 * count * rows * cols * width * 4,
            bytes_accessed=count * rows * cols * 4,
            transcendentals=0,
        ),
        name="project",
    )(*args)


def finish_kernel(own_ref, inverse_ref, first_ref, second_ref, out_ref, gram_ref):
    me = own_ref[1]
    gram = jnp.zeros_like(gram_ref)
    half = first_ref.shape[0]
    for i in range(half):
        for ref, place in ((first_ref, 2 * i), (second_ref, 2 * i + 1)):
            at = pl.multiple_of((place ^ me) * SLICE, SLICE)
            piece = jnp.dot(inverse_ref[...], ref[i], precision=high, preferred_element_type=f32)
            out_ref[:, pl.ds(at, SLICE)] = piece
            gram += lax.dot_general(
                piece, piece, (((1,), (1,)), ((), ())), precision=high, preferred_element_type=f32
            )
    gram_ref[...] = gram


def finish(own, inverse, evens, odds):
    half, width, _ = evens.shape
    return pl.pallas_call(
        finish_kernel,
        in_specs=[pl.BlockSpec(memory_space=pltpu.SMEM)] + [pl.BlockSpec(memory_space=pltpu.VMEM)] * 3,
        out_specs=[pl.BlockSpec(memory_space=pltpu.VMEM)] * 2,
        out_shape=[
            jax.ShapeDtypeStruct((width, 2 * half * SLICE), f32),
            jax.ShapeDtypeStruct((width, width), f32),
        ],
        compiler_params=pltpu.CompilerParams(vmem_limit_bytes=VMEM),
        name="finish",
    )(own, inverse, evens, odds)


CHUNKS = 2


def per_device(data, omega):
    nrow, ncol = lax.axis_size("row"), lax.axis_size("col")
    assert ncol == 4
    total_rows = data.shape[0] * nrow
    quarter = data.shape[0] // ncol
    slices = data.shape[1] // SLICE
    me_row = lax.axis_index("row")
    own = jnp.stack([lax.axis_index("col"), me_row % slices]).astype(jnp.int32)
    rows = quarter // CHUNKS

    owned = []
    for j in range(CHUNKS):
        send = partial_sketch(own, data, omega, (1, 3), j * rows, rows)
        keep = partial_sketch(own, data, omega, (0, 2), j * rows, rows)
        keep = keep + swap(send, "col", 1)
        owned.append(keep[0] + swap(keep[1], "col", 2))

    gram = sum(jnp.dot(v.T, v, precision=high, preferred_element_type=f32) for v in owned)
    bits = [1 << k for k in range(nrow.bit_length() - 1)]
    gram = gram + swap(gram, "col", 1)
    for bit in bits:
        gram = gram + swap(gram, "row", bit)
    gram = gram + swap(gram, "col", 2)

    second = [swap(v, "col", 1) for v in owned]
    third = [swap(v, "col", 2) for v in owned]
    fourth = [swap(v, "col", 1) for v in third]
    acc = None
    for j in range(CHUNKS):
        acc = project(own, data, [owned[j], second[j]], (0, 1), j * rows, acc)
    for j in range(CHUNKS):
        acc = project(own, data, [third[j], fourth[j]], (2, 3), j * rows, acc, j == CHUNKS - 1)
    send, keep = acc

    halving = [b for b in bits if b < slices]
    keep = keep + swap(send, "row", 1)
    for bit in reversed(halving[1:]):
        half = keep.shape[0] // 2
        keep = keep[:half] + swap(keep[half:], "row", bit)
    for bit in bits[len(halving) :]:
        keep = keep + swap(keep, "row", bit)
    for bit in halving[1:]:
        keep = jnp.concatenate([keep, swap(keep, "row", bit)], 0)
    other = swap(keep, "row", 1)

    lower = jnp.linalg.cholesky(gram)
    inverse = jax.scipy.linalg.solve_triangular(lower, jnp.eye(gram.shape[0], dtype=f32), lower=True)
    sketch = jnp.concatenate(owned, 0)
    basis = lax.dot_general(
        sketch, inverse, (((1,), (1,)), ((), ())), precision=high, preferred_element_type=f32
    )
    projected, small = finish(own, inverse, keep, other)
    small = small + swap(small, "col", 1)
    small = small + swap(small, "col", 2)
    return (basis, projected, small / total_rows)


def solution(mesh):
    placed = (P("row", "col"), P("col", None))
    return jax.shard_map(
        per_device,
        mesh=mesh,
        in_specs=placed,
        out_specs=(P(("row", "col"), None), P(None, "col"), P()),
        check_vma=False,
    )
```

```python
import jax
import jax.numpy as jnp
from jax import lax
from jax.sharding import PartitionSpec as P

full = lax.Precision.HIGHEST
three = lax.Precision.HIGH
f32 = jnp.float32

HALVES = 2


def swap(value, axis, bit):
    return lax.ppermute(value, axis, [(i, i ^ bit) for i in range(lax.axis_size(axis))])


def dot(a, b, a_dim, b_dim, precision=full):
    return lax.dot_general(
        a, b, (((a_dim,), (b_dim,)), ((), ())), precision=precision, preferred_element_type=f32
    )


def halves(value):
    rows = value.shape[0] // HALVES
    return [value[h * rows : (h + 1) * rows] for h in range(HALVES)]


def row_sum(value, me, bits, least=8):
    taken = []
    for bit in bits:
        rows = value.shape[0] // 2
        if rows < least:
            value = value + swap(value, "row", bit)
            continue
        mine = (me // bit) % 2
        send = lax.dynamic_slice_in_dim(value, (1 - mine) * rows, rows, 0)
        keep = lax.dynamic_slice_in_dim(value, mine * rows, rows, 0)
        value = keep + swap(send, "row", bit)
        taken.append(bit)
    for bit in reversed(taken):
        other = swap(value, "row", bit)
        mine = (me // bit) % 2
        value = jnp.where(
            mine == 0, jnp.concatenate([value, other], 0), jnp.concatenate([other, value], 0)
        )
    return value


def per_device(data, omega):
    nrow, ncol = lax.axis_size("row"), lax.axis_size("col")
    assert ncol == 4
    total_rows = data.shape[0] * nrow
    quarter = data.shape[0] // ncol
    me_row, me_col = lax.axis_index("row"), lax.axis_index("col")
    bits = [1 << k for k in range(nrow.bit_length() - 1)]

    places = [
        lax.dynamic_slice_in_dim(data, (me_col ^ q) * quarter, quarter, 0) for q in range(4)
    ]

    def part(q):
        return dot(omega, places[q], 0, 1, three)

    away = halves(part(2) + swap(part(3), "col", 1))
    away = [swap(v, "col", 2) for v in away]
    here = halves(part(0) + swap(part(1), "col", 1))
    owned = [a + b for a, b in zip(here, away)]
    turned = jnp.concatenate(owned, 0)

    gram = dot(turned, turned, 1, 1)
    gram = gram + swap(gram, "col", 1)
    for bit in bits:
        gram = gram + swap(gram, "row", bit)
    gram = gram + swap(gram, "col", 2)

    third = [swap(v, "col", 2) for v in owned]
    second = swap(turned, "col", 1)
    fourth = [swap(v, "col", 1) for v in third]
    near = halves(dot(turned, places[0], 1, 0, three) + dot(second, places[1], 1, 0, three))
    sums = []
    for h in range(HALVES):
        acc = near[h] + dot(third[h], places[2], 1, 0, three) + dot(fourth[h], places[3], 1, 0, three)
        sums.append(row_sum(acc, me_row, bits))
    raw = jnp.concatenate(sums, 0)

    lower = jnp.linalg.cholesky(gram)
    inverse = jax.scipy.linalg.solve_triangular(lower, jnp.eye(gram.shape[0], dtype=f32), lower=True)
    basis = dot(turned, inverse, 0, 1)
    projected = dot(inverse, raw, 1, 0)
    small = dot(projected, projected, 1, 1)
    small = small + swap(small, "col", 1)
    small = small + swap(small, "col", 2)
    return (basis, projected, small / total_rows)


def solution(mesh):
    placed = (P("row", "col"), P("col", None))
    return jax.shard_map(
        per_device,
        mesh=mesh,
        in_specs=placed,
        out_specs=(P(("row", "col"), None), P(None, "col"), P()),
        check_vma=False,
    )
```

```python
import jax
import jax.numpy as jnp
from jax import lax
from jax.sharding import PartitionSpec as P

full = lax.Precision.HIGHEST
three = lax.Precision.HIGH
f32 = jnp.float32

HALVES = 2


def swap(value, axis, bit):
    return lax.ppermute(value, axis, [(i, i ^ bit) for i in range(lax.axis_size(axis))])


def dot(a, b, a_dim, b_dim, precision=full):
    return lax.dot_general(
        a, b, (((a_dim,), (b_dim,)), ((), ())), precision=precision, preferred_element_type=f32
    )


def halves(value):
    rows = value.shape[0] // HALVES
    return [value[h * rows : (h + 1) * rows] for h in range(HALVES)]


def scatter_sum(value, axes):
    return jnp.sum(lax.all_to_all(value, axes, 0, 0), 0)


def spread(value, axes, count):
    return lax.all_to_all(jnp.broadcast_to(value[None], (count, *value.shape)), axes, 0, 0)


def small_sum(value, axes, count):
    rows = value.shape[0] // count
    mine = scatter_sum(value.reshape(count, rows, value.shape[1]), axes)
    return spread(mine, axes, count).reshape(value.shape)


def per_device(data, omega):
    nrow, ncol = lax.axis_size("row"), lax.axis_size("col")
    assert ncol == 4
    total_rows = data.shape[0] * nrow
    quarter = data.shape[0] // ncol
    me_col = lax.axis_index("col")

    places = [
        lax.dynamic_slice_in_dim(data, (me_col ^ q) * quarter, quarter, 0) for q in range(4)
    ]

    def part(q):
        return dot(omega, places[q], 0, 1, three)

    away = halves(part(2) + swap(part(3), "col", 1))
    away = [swap(v, "col", 2) for v in away]
    here = halves(part(0) + swap(part(1), "col", 1))
    owned = [a + b for a, b in zip(here, away)]
    turned = jnp.concatenate(owned, 0)

    gram = dot(turned, turned, 1, 1)
    gram = small_sum(gram, ("row", "col"), nrow * ncol)

    third = [swap(v, "col", 2) for v in owned]
    second = swap(turned, "col", 1)
    fourth = [swap(v, "col", 1) for v in third]
    near = halves(dot(turned, places[0], 1, 0, three) + dot(second, places[1], 1, 0, three))
    sums = []
    for h in range(HALVES):
        acc = near[h] + dot(third[h], places[2], 1, 0, three) + dot(fourth[h], places[3], 1, 0, three)
        cut = acc.reshape(acc.shape[0], nrow, -1).transpose(1, 0, 2)
        sums.append(scatter_sum(cut, "row"))
    raw = jnp.concatenate(sums, 0)

    lower = jnp.linalg.cholesky(gram)
    inverse = jax.scipy.linalg.solve_triangular(lower, jnp.eye(gram.shape[0], dtype=f32), lower=True)
    basis = dot(turned, inverse, 0, 1)
    own_part = dot(inverse, raw, 1, 0)
    small = small_sum(dot(own_part, own_part, 1, 1), ("row", "col"), nrow * ncol)
    spreaded = spread(own_part, "row", nrow)
    projected = spreaded.transpose(1, 0, 2).reshape(raw.shape[0], data.shape[1])
    return (basis, projected, small / total_rows)


def solution(mesh):
    placed = (P("row", "col"), P("col", None))
    return jax.shard_map(
        per_device,
        mesh=mesh,
        in_specs=placed,
        out_specs=(P(("row", "col"), None), P(None, "col"), P()),
        check_vma=False,
    )
```

```python
import functools

import jax
import jax.numpy as jnp
from jax import lax
from jax.experimental import pallas as pl
from jax.experimental.pallas import tpu as pltpu
from jax.sharding import PartitionSpec as P

full = lax.Precision.HIGHEST
f32 = jnp.float32
bf16 = jnp.bfloat16

PIECE = 512
TILE = 256
SMEM = pl.BlockSpec(memory_space=pltpu.SMEM)
VMEM = pl.BlockSpec(memory_space=pltpu.VMEM)
ANY = pl.BlockSpec(memory_space=pl.ANY)
FREE = pl.CostEstimate(flops=1, bytes_accessed=1, transcendentals=0)


def params(mib):
    return pltpu.CompilerParams(vmem_limit_bytes=mib * 1024 * 1024)


def swap(value, axis, bit):
    return lax.ppermute(value, axis, [(i, i ^ bit) for i in range(lax.axis_size(axis))])


def dot(a, b, a_dim, b_dim, precision=full):
    return lax.dot_general(
        a, b, (((a_dim,), (b_dim,)), ((), ())), precision=precision, preferred_element_type=f32
    )


def split(value):
    upper = value.astype(bf16)
    return upper, (value - upper.astype(f32)).astype(bf16)


def start_copies(own_ref, data_ref, held, sems, pieces, quarter):
    copies = []
    for k, (place, first) in enumerate(pieces):
        at = pl.multiple_of((own_ref[0] ^ place) * quarter + first, PIECE)
        row = []
        for t in range(data_ref.shape[1] // TILE):
            cols = pl.ds(t * TILE, TILE)
            copy = pltpu.make_async_copy(
                data_ref.at[pl.ds(at, PIECE), cols], held.at[k, :, cols], sems.at[k, t]
            )
            copy.start()
            row.append(copy)
        copies.append(row)
    return copies


def sketch_kernel(pieces, quarter, first, own_ref, data_ref, omega_ref, *refs):
    outs, (held, sems) = refs[:-2], refs[-2:]
    copies = start_copies(own_ref, data_ref, held, sems, pieces, quarter)
    if first:
        width = omega_ref.shape[1]
        wide = outs[-1]
        upper, rest = split(omega_ref[...])
        wide[:, :width] = upper
        wide[:, width:] = rest
    else:
        wide = omega_ref
        width = omega_ref.shape[1] // 2
    for k in range(len(pieces)):
        both = more = None
        for t, copy in enumerate(copies[k]):
            copy.wait()
            upper, rest = split(held[k, :, t * TILE : (t + 1) * TILE])
            omega = wide[t * TILE : (t + 1) * TILE, :]
            one = jnp.dot(upper, omega, preferred_element_type=f32)
            two = jnp.dot(rest, omega[:, :width], preferred_element_type=f32)
            both = one if both is None else both + one
            more = two if more is None else more + two
        outs[k][...] = both[:, :width] + both[:, width:] + more


def sketch(own, data, omega, pieces, first=False):
    cols = data.shape[1]
    width = omega.shape[1] if first else omega.shape[1] // 2
    quarter = data.shape[0] // lax.axis_size("col")
    out = [jax.ShapeDtypeStruct((PIECE, width), f32)] * len(pieces)
    if first:
        out.append(jax.ShapeDtypeStruct((cols, 2 * width), bf16))
    return pl.pallas_call(
        functools.partial(sketch_kernel, pieces, quarter, first),
        in_specs=[SMEM, ANY, VMEM],
        out_specs=[VMEM] * len(out),
        out_shape=out,
        scratch_shapes=[
            pltpu.VMEM((len(pieces), PIECE, cols), f32),
            pltpu.SemaphoreType.DMA((len(pieces), cols // TILE)),
        ],
        compiler_params=params(20),
        cost_estimate=FREE,
        name="partial_sketch",
    )(own, data, omega)


def order(bits):
    places = [0]
    for bit in reversed(bits):
        places = places + [place ^ bit for place in places]
    return places


def project_kernel(pieces, quarter, before, orders, own_ref, data_ref, *refs):
    count = len(pieces)
    parts, refs = refs[:count], refs[count:]
    old, refs = (refs[0], refs[1:]) if before else (None, refs)
    outs, (total, held, sems) = refs[:-3], refs[-3:]
    if orders is None:
        total = outs[0]
    copies = start_copies(own_ref, data_ref, held, sems, pieces, quarter)
    for k in range(count):
        upper, rest = split(parts[k][...].T)
        stack = jnp.concatenate([upper, rest], 0)
        width = upper.shape[0]
        for t, copy in enumerate(copies[k]):
            copy.wait()
            cols = slice(t * TILE, (t + 1) * TILE)
            d_upper, d_rest = split(held[k, :, cols])
            both = jnp.dot(stack, d_upper, preferred_element_type=f32)
            value = both[:width] + both[width:] + jnp.dot(upper, d_rest, preferred_element_type=f32)
            if k > 0:
                value += total[:, cols]
            elif before:
                value += old[:, cols]
            total[:, cols] = value
    if orders is not None:
        for piece, places in enumerate(orders):
            send, keep = outs[2 * piece], outs[2 * piece + 1]
            half = len(places) // 2
            step = send.shape[0] // half
            for i in range(half):
                for ref, place in ((keep, places[i]), (send, places[half + i])):
                    at = piece * 2 * half * step + (place ^ own_ref[1]) * step
                    ref[i * step : (i + 1) * step] = total[pl.ds(pl.multiple_of(at, step), step)]


def project(own, data, pieces, parts, before=None, orders=None):
    cols = data.shape[1]
    width = parts[0].shape[1]
    quarter = data.shape[0] // lax.axis_size("col")
    args = [own, data, *parts] + ([] if before is None else [before])
    if orders is None:
        out = [jax.ShapeDtypeStruct((width, cols), f32)]
    else:
        out = [jax.ShapeDtypeStruct((width // len(orders) // 2, cols), f32)] * (2 * len(orders))
    return pl.pallas_call(
        functools.partial(project_kernel, pieces, quarter, before is not None, orders),
        in_specs=[SMEM, ANY] + [VMEM] * (len(args) - 2),
        out_specs=[VMEM] * len(out),
        out_shape=out,
        scratch_shapes=[
            pltpu.VMEM((width, cols) if orders is not None else (8, 128), f32),
            pltpu.VMEM((len(pieces), PIECE, cols), f32),
            pltpu.SemaphoreType.DMA((len(pieces), cols // TILE)),
        ],
        compiler_params=params(24),
        cost_estimate=FREE,
        name="project",
    )(*args)


def factor_kernel(gram_ref, out_ref, work):
    n = gram_ref.shape[0]
    row = lax.broadcasted_iota(jnp.int32, (n, n), 0)
    col = lax.broadcasted_iota(jnp.int32, (n, n), 1)
    work[:, :n] = gram_ref[...]
    work[:, n:] = jnp.where(row == col, 1.0, 0.0).astype(f32)
    sub = lax.broadcasted_iota(jnp.int32, (8, n), 0)
    for b in range(n // 8):
        top = slice(8 * b, 8 * b + 8)
        panel = work[top, :]
        spread = [jnp.broadcast_to(panel[:, 8 * b + j : 8 * b + j + 1], (8, n)) for j in range(8)]
        e = [
            [jnp.broadcast_to(spread[j][i : i + 1, :], (8, n)) for j in range(i + 1)]
            for i in range(8)
        ]
        left = [jnp.broadcast_to(panel[i : i + 1, :n], (8, n)) for i in range(8)]
        right = [jnp.broadcast_to(panel[i : i + 1, n:], (8, n)) for i in range(8)]
        for j in range(8):
            scale = lax.rsqrt(e[j][j])
            left[j] = left[j] * scale
            right[j] = right[j] * scale
            low = {i: e[i][j] * scale for i in range(j + 1, 8)}
            for i in range(j + 1, 8):
                for k in range(j + 1, i + 1):
                    e[i][k] = e[i][k] - low[i] * low[k]
                left[i] = left[i] - low[i] * left[j]
                right[i] = right[i] - low[i] * right[j]
        l_panel, r_panel = left[0], right[0]
        for i in range(1, 8):
            l_panel = jnp.where(sub == i, left[i], l_panel)
            r_panel = jnp.where(sub == i, right[i], r_panel)
        out_ref[top, :] = r_panel
        if b < n // 8 - 1:
            done = jnp.concatenate([l_panel, r_panel], 1)
            change = dot(l_panel, done, 0, 0)
            below = slice(8 * b + 8, n)
            work[below, :] = work[below, :] - change[8 * b + 8 :, :]


def factor(gram):
    n = gram.shape[0]
    return pl.pallas_call(
        factor_kernel,
        in_specs=[VMEM],
        out_specs=VMEM,
        out_shape=jax.ShapeDtypeStruct((n, n), f32),
        scratch_shapes=[pltpu.VMEM((n, 2 * n), f32)],
        compiler_params=params(8),
        cost_estimate=FREE,
        name="factor",
    )(gram)


def finish_kernel(orders, own_ref, inverse_ref, *refs):
    count = 2 * len(orders)
    parts, (out_ref, gram_ref, total) = refs[:count], refs[count:]
    for piece, places in enumerate(orders):
        keep, other = parts[2 * piece], parts[2 * piece + 1]
        half = len(places) // 2
        step = keep.shape[0] // half
        for i in range(half):
            for ref, place in ((keep, places[i]), (other, places[half + i])):
                at = piece * 2 * half * step + (place ^ own_ref[1]) * step
                total[pl.ds(pl.multiple_of(at, step), step)] = ref[i * step : (i + 1) * step]
    value = jnp.dot(inverse_ref[...], total[...], precision=full, preferred_element_type=f32)
    out_ref[...] = value
    gram_ref[...] = dot(value, value, 1, 1)


def finish(own, inverse, parts, orders):
    width = inverse.shape[0]
    cols = parts[0].shape[1]
    return pl.pallas_call(
        functools.partial(finish_kernel, orders),
        in_specs=[SMEM] + [VMEM] * (1 + len(parts)),
        out_specs=[VMEM] * 2,
        out_shape=[
            jax.ShapeDtypeStruct((width, cols), f32),
            jax.ShapeDtypeStruct((width, width), f32),
        ],
        scratch_shapes=[pltpu.VMEM((width, cols), f32)],
        compiler_params=params(16),
        cost_estimate=FREE,
        name="finish",
    )(own, inverse, *parts)


def per_device(data, omega):
    nrow, ncol = lax.axis_size("row"), lax.axis_size("col")
    quarter = data.shape[0] // ncol
    assert ncol == 4 and quarter == 2 * PIECE and nrow >= 8
    total_rows = data.shape[0] * nrow
    own = jnp.stack([lax.axis_index("col"), lax.axis_index("row") % 8]).astype(jnp.int32)
    bits = [1 << k for k in range(nrow.bit_length() - 1)]

    a3, wide = sketch(own, data, omega, [(3, 0)], True)
    (a2,) = sketch(own, data, wide, [(2, 0)])
    away_a = swap(a2 + swap(a3, "col", 1), "col", 2)
    (b3,) = sketch(own, data, wide, [(3, PIECE)])
    (b2,) = sketch(own, data, wide, [(2, PIECE)])
    away_b = swap(b2 + swap(b3, "col", 1), "col", 2)
    a1, b1 = sketch(own, data, wide, [(1, 0), (1, PIECE)])
    a0, b0 = sketch(own, data, wide, [(0, 0), (0, PIECE)])
    own_a = a0 + swap(a1, "col", 1) + away_a
    own_b = b0 + swap(b1, "col", 1) + away_b

    third_a = swap(own_a, "col", 2)
    third_b = swap(own_b, "col", 2)
    second_a = swap(own_a, "col", 1)
    second_b = swap(own_b, "col", 1)
    fourth_a = swap(third_a, "col", 1)
    fourth_b = swap(third_b, "col", 1)

    gram = dot(own_a, own_a, 0, 0) + dot(own_b, own_b, 0, 0)
    gram = gram + swap(gram, "col", 1)
    for bit in bits:
        gram = gram + swap(gram, "row", bit)
    gram = gram + swap(gram, "col", 2)
    inverse = factor(gram)
    basis = dot(jnp.concatenate([own_a, own_b], 0), inverse, 1, 1)

    cuts = [(1, 2, 4), (2, 4, 1)]
    orders = [order(cut) for cut in cuts]
    (acc,) = project(
        own, data, [(0, 0), (1, 0), (0, PIECE), (1, PIECE)], [own_a, second_a, own_b, second_b]
    )
    (acc,) = project(own, data, [(2, 0), (3, 0)], [third_a, fourth_a], acc)
    sums = project(own, data, [(2, PIECE), (3, PIECE)], [third_b, fourth_b], acc, orders)

    parts = []
    for piece, cut in enumerate(cuts):
        send, keep = sums[2 * piece], sums[2 * piece + 1]
        for k, bit in enumerate(cut):
            if k > 0:
                half = keep.shape[0] // 2
                keep, send = keep[:half], keep[half:]
            keep = keep + swap(send, "row", bit)
        for bit in bits[3:]:
            keep = keep + swap(keep, "row", bit)
        for bit in reversed(cut[1:]):
            keep = jnp.concatenate([keep, swap(keep, "row", bit)], 0)
        parts += [keep, swap(keep, "row", cut[0])]

    projected, small = finish(own, inverse, parts, orders)
    small = small + swap(small, "col", 1)
    small = small + swap(small, "col", 2)
    return (basis, projected, small / total_rows)


def solution(mesh):
    placed = (P("row", "col"), P("col", None))
    return jax.shard_map(
        per_device,
        mesh=mesh,
        in_specs=placed,
        out_specs=(P(("row", "col"), None), P(None, "col"), P()),
        check_vma=False,
    )
```

```python
import functools

import jax
import jax.numpy as jnp
from jax import lax
from jax.experimental import pallas as pl
from jax.experimental.pallas import tpu as pltpu
from jax.sharding import PartitionSpec as P

full = lax.Precision.HIGHEST
f32 = jnp.float32
bf16 = jnp.bfloat16

PIECE = 512
TILE = 256
SMEM = pl.BlockSpec(memory_space=pltpu.SMEM)
VMEM = pl.BlockSpec(memory_space=pltpu.VMEM)
HBM = pl.BlockSpec(memory_space=pltpu.HBM)
fence = lax.optimization_barrier


def cost(mib):
    return pl.CostEstimate(flops=1, bytes_accessed=int(mib * 2**20), transcendentals=0)


def params():
    return pltpu.CompilerParams(vmem_limit_bytes=52 * 1024 * 1024)


def swap(value, axis, bit):
    return lax.ppermute(value, axis, [(i, i ^ bit) for i in range(lax.axis_size(axis))])


def dot(a, b, a_dim, b_dim, precision=full):
    return lax.dot_general(
        a, b, (((a_dim,), (b_dim,)), ((), ())), precision=precision, preferred_element_type=f32
    )


def split(value):
    upper = value.astype(bf16)
    return upper, (value - upper.astype(f32)).astype(bf16)


def start_copies(own_ref, data_ref, held, sems, pieces, quarter):
    copies = []
    for k, (place, first) in enumerate(pieces):
        at = pl.multiple_of((own_ref[0] ^ place) * quarter + first, PIECE)
        row = []
        for t in range(data_ref.shape[1] // TILE):
            cols = pl.ds(t * TILE, TILE)
            copy = pltpu.make_async_copy(
                data_ref.at[pl.ds(at, PIECE), cols], held.at[k, :, cols], sems.at[k, t]
            )
            copy.start()
            row.append(copy)
        copies.append(row)
    return copies


def sketch_kernel(pieces, quarter, first, own_ref, data_ref, omega_ref, *refs):
    if first:
        refs, (omega_held, omega_sem) = refs[:-2], refs[-2:]
        omega_copy = pltpu.make_async_copy(omega_ref, omega_held, omega_sem)
        omega_copy.start()
    outs, (held, sems) = refs[:-2], refs[-2:]
    copies = start_copies(own_ref, data_ref, held, sems, pieces, quarter)
    if first:
        width = omega_ref.shape[1]
        wide = outs[-1]
        omega_copy.wait()
        upper, rest = split(omega_held[...])
        wide[:, :width] = upper
        wide[:, width:] = rest
    else:
        wide = omega_ref
        width = omega_ref.shape[1] // 2
    for k in range(len(pieces)):
        both = more = None
        for t, copy in enumerate(copies[k]):
            copy.wait()
            upper, rest = split(held[k, :, t * TILE : (t + 1) * TILE])
            omega = wide[t * TILE : (t + 1) * TILE, :]
            one = jnp.dot(upper, omega, preferred_element_type=f32)
            two = jnp.dot(rest, omega[:, :width], preferred_element_type=f32)
            both = one if both is None else both + one
            more = two if more is None else more + two
        first_row = pieces[k][1]
        out = outs[k // 2]
        out[first_row : first_row + PIECE] = both[:, :width] + both[:, width:] + more


def sketch(own, data, omega, places, first=False):
    pieces = [(place, row) for place in places for row in (0, PIECE)]
    cols = data.shape[1]
    width = omega.shape[1] if first else omega.shape[1] // 2
    quarter = data.shape[0] // lax.axis_size("col")
    out = [jax.ShapeDtypeStruct((quarter, width), f32)] * len(places)
    if first:
        out.append(jax.ShapeDtypeStruct((cols, 2 * width), bf16))
    scratch = [
        pltpu.VMEM((len(pieces), PIECE, cols), f32),
        pltpu.SemaphoreType.DMA((len(pieces), cols // TILE)),
    ]
    if first:
        scratch += [pltpu.VMEM(omega.shape, f32), pltpu.SemaphoreType.DMA]
    return pl.pallas_call(
        functools.partial(sketch_kernel, pieces, quarter, first),
        in_specs=[SMEM, HBM, HBM if first else VMEM],
        out_specs=[VMEM] * len(out),
        out_shape=out,
        scratch_shapes=scratch,
        compiler_params=params(),
        cost_estimate=cost(0.01 * len(pieces)),
        name="partial_sketch",
    )(own, data, omega)


def order(bits):
    places = [0]
    for bit in reversed(bits):
        places = places + [place ^ bit for place in places]
    return places


def project_kernel(pieces, quarter, before, orders, own_ref, data_ref, *refs):
    count = len(pieces)
    parts, refs = refs[: count // 2], refs[count // 2 :]
    old, refs = (refs[0], refs[1:]) if before else (None, refs)
    outs, (total, held, sems) = refs[:-3], refs[-3:]
    if orders is None:
        total = outs[0]
    copies = start_copies(own_ref, data_ref, held, sems, pieces, quarter)
    for k in range(count):
        first = pieces[k][1]
        upper, rest = split(parts[k // 2][first : first + PIECE].T)
        stack = jnp.concatenate([upper, rest], 0)
        width = upper.shape[0]
        for t, copy in enumerate(copies[k]):
            copy.wait()
            cols = slice(t * TILE, (t + 1) * TILE)
            d_upper, d_rest = split(held[k, :, cols])
            both = jnp.dot(stack, d_upper, preferred_element_type=f32)
            value = both[:width] + both[width:] + jnp.dot(upper, d_rest, preferred_element_type=f32)
            if k > 0:
                value += total[:, cols]
            elif before:
                value += old[:, cols]
            total[:, cols] = value
    if orders is not None:
        for piece, places in enumerate(orders):
            send, keep = outs[2 * piece], outs[2 * piece + 1]
            half = len(places) // 2
            step = send.shape[0] // half
            for i in range(half):
                for ref, place in ((keep, places[i]), (send, places[half + i])):
                    at = piece * 2 * half * step + (place ^ own_ref[1]) * step
                    ref[i * step : (i + 1) * step] = total[pl.ds(pl.multiple_of(at, step), step)]


def project(own, data, places, parts, before=None, orders=None):
    pieces = [(place, first) for place in places for first in (0, PIECE)]
    cols = data.shape[1]
    width = parts[0].shape[1]
    quarter = data.shape[0] // lax.axis_size("col")
    args = [own, data, *parts] + ([] if before is None else [before])
    if orders is None:
        out = [jax.ShapeDtypeStruct((width, cols), f32)]
    else:
        out = [jax.ShapeDtypeStruct((width // len(orders) // 2, cols), f32)] * (2 * len(orders))
    return pl.pallas_call(
        functools.partial(project_kernel, pieces, quarter, before is not None, orders),
        in_specs=[SMEM, HBM] + [VMEM] * (len(args) - 2),
        out_specs=[VMEM] * len(out),
        out_shape=out,
        scratch_shapes=[
            pltpu.VMEM((width, cols) if orders is not None else (8, 128), f32),
            pltpu.VMEM((len(pieces), PIECE, cols), f32),
            pltpu.SemaphoreType.DMA((len(pieces), cols // TILE)),
        ],
        compiler_params=params(),
        cost_estimate=cost(6 * len(pieces)),
        name="project",
    )(*args)


def factor_kernel(index, count, in_ref, out_ref, *scratch):
    n = in_ref.shape[0]
    last = index == count - 1
    work = scratch[0] if last else out_ref
    if index == 0:
        row = lax.broadcasted_iota(jnp.int32, (n, n), 0)
        col = lax.broadcasted_iota(jnp.int32, (n, n), 1)
        work[:, :n] = in_ref[...]
        work[:, n:] = jnp.where(row == col, 1.0, 0.0).astype(f32)
    else:
        work[...] = in_ref[...]
    sub = lax.broadcasted_iota(jnp.int32, (8, n), 0)
    panels = n // 8
    for b in range(panels * index // count, panels * (index + 1) // count):
        top = slice(8 * b, 8 * b + 8)
        panel = work[top, :]
        spread = [jnp.broadcast_to(panel[:, 8 * b + j : 8 * b + j + 1], (8, n)) for j in range(8)]
        e = [
            [jnp.broadcast_to(spread[j][i : i + 1, :], (8, n)) for j in range(i + 1)]
            for i in range(8)
        ]
        left = [jnp.broadcast_to(panel[i : i + 1, :n], (8, n)) for i in range(8)]
        right = [jnp.broadcast_to(panel[i : i + 1, n:], (8, n)) for i in range(8)]
        for j in range(8):
            scale = lax.rsqrt(e[j][j])
            left[j] = left[j] * scale
            right[j] = right[j] * scale
            low = {i: e[i][j] * scale for i in range(j + 1, 8)}
            for i in range(j + 1, 8):
                for k in range(j + 1, i + 1):
                    e[i][k] = e[i][k] - low[i] * low[k]
                left[i] = left[i] - low[i] * left[j]
                right[i] = right[i] - low[i] * right[j]
        l_panel, r_panel = left[0], right[0]
        for i in range(1, 8):
            l_panel = jnp.where(sub == i, left[i], l_panel)
            r_panel = jnp.where(sub == i, right[i], r_panel)
        work[top, n:] = r_panel
        if b < panels - 1:
            done = jnp.concatenate([l_panel, r_panel], 1)
            change = dot(l_panel, done, 0, 0)
            below = slice(8 * b + 8, n)
            work[below, :] = work[below, :] - change[8 * b + 8 :, :]
    if last:
        out_ref[...] = work[:, n:]


def factor(index, count, value):
    n = value.shape[0]
    last = index == count - 1
    return pl.pallas_call(
        functools.partial(factor_kernel, index, count),
        in_specs=[VMEM],
        out_specs=VMEM,
        out_shape=jax.ShapeDtypeStruct((n, n if last else 2 * n), f32),
        scratch_shapes=[pltpu.VMEM((n, 2 * n), f32)] if last else [],
        compiler_params=params(),
        cost_estimate=cost(32 / count),
        name="factor",
    )(value)


def finish_kernel(orders, own_ref, inverse_ref, *refs):
    count = 2 * len(orders)
    parts, (out_ref, gram_ref, total) = refs[:count], refs[count:]
    for piece, places in enumerate(orders):
        keep, other = parts[2 * piece], parts[2 * piece + 1]
        half = len(places) // 2
        step = keep.shape[0] // half
        for i in range(half):
            for ref, place in ((keep, places[i]), (other, places[half + i])):
                at = piece * 2 * half * step + (place ^ own_ref[1]) * step
                total[pl.ds(pl.multiple_of(at, step), step)] = ref[i * step : (i + 1) * step]
    value = jnp.dot(inverse_ref[...], total[...], precision=full, preferred_element_type=f32)
    out_ref[...] = value
    gram_ref[...] = dot(value, value, 1, 1)


def finish(own, inverse, parts, orders):
    width = inverse.shape[0]
    cols = parts[0].shape[1]
    return pl.pallas_call(
        functools.partial(finish_kernel, orders),
        in_specs=[SMEM] + [VMEM] * (1 + len(parts)),
        out_specs=[VMEM] * 2,
        out_shape=[
            jax.ShapeDtypeStruct((width, cols), f32),
            jax.ShapeDtypeStruct((width, width), f32),
        ],
        scratch_shapes=[pltpu.VMEM((width, cols), f32)],
        compiler_params=params(),
        cost_estimate=cost(8),
        name="finish",
    )(own, inverse, *parts)


def per_device(data, omega):
    nrow, ncol = lax.axis_size("row"), lax.axis_size("col")
    quarter = data.shape[0] // ncol
    assert ncol == 4 and quarter == 2 * PIECE and nrow >= 8
    total_rows = data.shape[0] * nrow
    own = jnp.stack([lax.axis_index("col"), lax.axis_index("row") % 8]).astype(jnp.int32)
    bits = [1 << k for k in range(nrow.bit_length() - 1)]

    part, wide = sketch(own, data, omega, [3], True)
    (pair,) = sketch(own, data, wide, [2])
    pair, wide = fence((pair + swap(part, "col", 1), wide))
    away = swap(pair, "col", 2)
    part, here = sketch(own, data, wide, [1, 0])
    part, away = fence((swap(part, "col", 1), away))
    sketched = here + part + away

    third = swap(sketched, "col", 2)
    second = swap(sketched, "col", 1)
    gram = dot(sketched, sketched, 0, 0)
    gram = gram + swap(gram, "row", bits[0])
    (acc,) = project(own, data, [0], [sketched])
    gram, acc, second = fence((gram, acc, second))
    gram = gram + swap(gram, "row", bits[1])
    (acc,) = project(own, data, [1], [second], acc)
    gram, acc = fence((gram, acc))
    for bit in bits[2:]:
        gram = gram + swap(gram, "row", bit)
    gram = gram + swap(gram, "col", 1)
    third, gram, acc = fence((third, gram, acc))
    fourth = swap(third, "col", 1)
    gram = gram + swap(gram, "col", 2)
    (acc,) = project(own, data, [2], [third], acc)
    gram, acc, fourth = fence((gram, acc, fourth))
    cuts = [(1, 2, 4), (2, 4, 1)]
    orders = [order(cut) for cut in cuts]
    sums = project(own, data, [3], [fourth], acc, orders)

    *sums, state = fence((*sums, gram))
    sends, keeps = sums[0::2], sums[1::2]
    for k in range(3):
        if k > 0:
            half = keeps[0].shape[0] // 2
            sends, keeps = [v[half:] for v in keeps], [v[:half] for v in keeps]
        keeps = [v + swap(w, "row", cut[k]) for v, w, cut in zip(keeps, sends, cuts)]
        state = factor(k, 4, state)
        *keeps, state = fence((*keeps, state))
    for bit in bits[3:]:
        keeps = [v + swap(v, "row", bit) for v in keeps]
    keeps = [jnp.concatenate([v, swap(v, "row", cut[2])], 0) for v, cut in zip(keeps, cuts)]
    inverse = factor(3, 4, state)
    *keeps, inverse = fence((*keeps, inverse))
    keeps = [jnp.concatenate([v, swap(v, "row", cut[1])], 0) for v, cut in zip(keeps, cuts)]
    basis = dot(sketched, inverse, 1, 1)
    *keeps, basis = fence((*keeps, basis))
    parts = []
    for v, cut in zip(keeps, cuts):
        parts += [v, swap(v, "row", cut[0])]

    projected, small = finish(own, inverse, parts, orders)
    small = small + swap(small, "col", 1)
    small = small + swap(small, "col", 2)
    return (basis, projected, small / total_rows)


def solution(mesh):
    placed = (P("row", "col"), P("col", None))
    return jax.shard_map(
        per_device,
        mesh=mesh,
        in_specs=placed,
        out_specs=(P(("row", "col"), None), P(None, "col"), P()),
        check_vma=False,
    )
```

```python
import functools

import jax
import jax.numpy as jnp
from jax import lax
from jax.experimental import pallas as pl
from jax.experimental.pallas import tpu as pltpu
from jax.sharding import PartitionSpec as P

full = lax.Precision.HIGHEST
f32 = jnp.float32
bf16 = jnp.bfloat16

PIECE = 512
TILE = 256
SMEM = pl.BlockSpec(memory_space=pltpu.SMEM)
VMEM = pl.BlockSpec(memory_space=pltpu.VMEM)
HBM = pl.BlockSpec(memory_space=pltpu.HBM)
fence = lax.optimization_barrier


def cost(mib):
    return pl.CostEstimate(flops=1, bytes_accessed=int(mib * 2**20), transcendentals=0)


def params():
    return pltpu.CompilerParams(vmem_limit_bytes=16 * 1024 * 1024)


def swap(value, axis, bit):
    return lax.ppermute(value, axis, [(i, i ^ bit) for i in range(lax.axis_size(axis))])


def dot(a, b, a_dim, b_dim, precision=full):
    return lax.dot_general(
        a, b, (((a_dim,), (b_dim,)), ((), ())), precision=precision, preferred_element_type=f32
    )


def split(value):
    upper = value.astype(bf16)
    return upper, (value - upper.astype(f32)).astype(bf16)


def rows_of(own_ref, piece, quarter):
    place, first = piece
    return pl.ds(pl.multiple_of((own_ref[0] ^ place) * quarter + first, PIECE), PIECE)


def start_copies(own_ref, data_ref, held, sems, pieces, quarter):
    copies = []
    for k, piece in enumerate(pieces):
        row = []
        for t in range(data_ref.shape[1] // TILE):
            cols = pl.ds(t * TILE, TILE)
            copy = pltpu.make_async_copy(
                data_ref.at[rows_of(own_ref, piece, quarter), cols], held.at[k, :, cols], sems.at[k, t]
            )
            copy.start()
            row.append(copy)
        copies.append(row)
    return copies


def sketch_kernel(pieces, quarter, first, near, own_ref, data_ref, omega_ref, *refs):
    if first:
        refs, (omega_held, omega_sem) = refs[:-2], refs[-2:]
        omega_copy = pltpu.make_async_copy(omega_ref, omega_held, omega_sem)
        omega_copy.start()
    if near:
        outs, copies = refs, None
    else:
        outs, (held, sems) = refs[:-2], refs[-2:]
        copies = start_copies(own_ref, data_ref, held, sems, pieces, quarter)
    if first:
        width = omega_ref.shape[1]
        wide = outs[-1]
        omega_copy.wait()
        upper, rest = split(omega_held[...])
        wide[:, :width] = upper
        wide[:, width:] = rest
    else:
        wide = omega_ref
        width = omega_ref.shape[1] // 2
    for k in range(len(pieces)):
        both = more = None
        for t in range(data_ref.shape[1] // TILE):
            if near:
                value = data_ref[rows_of(own_ref, pieces[k], quarter), t * TILE : (t + 1) * TILE]
            else:
                copies[k][t].wait()
                value = held[k, :, t * TILE : (t + 1) * TILE]
            upper, rest = split(value)
            omega = wide[t * TILE : (t + 1) * TILE, :]
            one = jnp.dot(upper, omega, preferred_element_type=f32)
            two = jnp.dot(rest, omega[:, :width], preferred_element_type=f32)
            both = one if both is None else both + one
            more = two if more is None else more + two
        first_row = pieces[k][1]
        out = outs[k // 2]
        out[first_row : first_row + PIECE] = both[:, :width] + both[:, width:] + more


def sketch(own, data, omega, places, first=False, near=False):
    pieces = [(place, row) for place in places for row in (0, PIECE)]
    cols = data.shape[1]
    width = omega.shape[1] if first else omega.shape[1] // 2
    quarter = data.shape[0] // lax.axis_size("col")
    out = [jax.ShapeDtypeStruct((quarter, width), f32)] * len(places)
    if first:
        out.append(jax.ShapeDtypeStruct((cols, 2 * width), bf16))
    scratch = [
        pltpu.VMEM((len(pieces), PIECE, cols), f32),
        pltpu.SemaphoreType.DMA((len(pieces), cols // TILE)),
    ]
    if near:
        scratch = []
    if first:
        scratch += [pltpu.VMEM(omega.shape, f32), pltpu.SemaphoreType.DMA]
    return pl.pallas_call(
        functools.partial(sketch_kernel, pieces, quarter, first, near),
        in_specs=[SMEM, VMEM if near else HBM, HBM if first else VMEM],
        out_specs=[VMEM] * len(out),
        out_shape=out,
        scratch_shapes=scratch,
        compiler_params=params(),
        cost_estimate=cost(0.01 * len(pieces)),
        name="partial_sketch",
    )(own, data, omega)


def order(bits):
    places = [0]
    for bit in reversed(bits):
        places = places + [place ^ bit for place in places]
    return places


def project_kernel(pieces, quarter, before, orders, own_ref, data_ref, *refs):
    count = len(pieces)
    parts, refs = refs[: count // 2], refs[count // 2 :]
    old, refs = (refs[0], refs[1:]) if before else (None, refs)
    outs, total = (refs, refs[0]) if orders is None else (refs[:-1], refs[-1])
    for k in range(count):
        first = pieces[k][1]
        upper, rest = split(parts[k // 2][first : first + PIECE].T)
        stack = jnp.concatenate([upper, rest], 0)
        width = upper.shape[0]
        for t in range(data_ref.shape[1] // TILE):
            cols = slice(t * TILE, (t + 1) * TILE)
            d_upper, d_rest = split(data_ref[rows_of(own_ref, pieces[k], quarter), cols])
            both = jnp.dot(stack, d_upper, preferred_element_type=f32)
            value = both[:width] + both[width:] + jnp.dot(upper, d_rest, preferred_element_type=f32)
            if k > 0:
                value += total[:, cols]
            elif before:
                value += old[:, cols]
            total[:, cols] = value
    if orders is not None:
        for piece, places in enumerate(orders):
            send, keep = outs[2 * piece], outs[2 * piece + 1]
            half = len(places) // 2
            step = send.shape[0] // half
            for i in range(half):
                for ref, place in ((keep, places[i]), (send, places[half + i])):
                    at = piece * 2 * half * step + (place ^ own_ref[1]) * step
                    ref[i * step : (i + 1) * step] = total[pl.ds(pl.multiple_of(at, step), step)]


def project(own, data, places, parts, before=None, orders=None):
    pieces = [(place, first) for place in places for first in (0, PIECE)]
    cols = data.shape[1]
    width = parts[0].shape[1]
    quarter = data.shape[0] // lax.axis_size("col")
    args = [own, data, *parts] + ([] if before is None else [before])
    if orders is None:
        out = [jax.ShapeDtypeStruct((width, cols), f32)]
    else:
        out = [jax.ShapeDtypeStruct((width // len(orders) // 2, cols), f32)] * (2 * len(orders))
    return pl.pallas_call(
        functools.partial(project_kernel, pieces, quarter, before is not None, orders),
        in_specs=[SMEM] + [VMEM] * (len(args) - 1),
        out_specs=[VMEM] * len(out),
        out_shape=out,
        scratch_shapes=[] if orders is None else [pltpu.VMEM((width, cols), f32)],
        compiler_params=params(),
        cost_estimate=cost(6 * len(pieces)),
        name="project",
    )(*args)


def factor_kernel(index, count, in_ref, out_ref, *scratch):
    n = in_ref.shape[0]
    last = index == count - 1
    work = scratch[0] if last else out_ref
    if index == 0:
        row = lax.broadcasted_iota(jnp.int32, (n, n), 0)
        col = lax.broadcasted_iota(jnp.int32, (n, n), 1)
        work[:, :n] = in_ref[...]
        work[:, n:] = jnp.where(row == col, 1.0, 0.0).astype(f32)
    else:
        work[...] = in_ref[...]
    sub = lax.broadcasted_iota(jnp.int32, (8, n), 0)
    panels = n // 8
    for b in range(panels * index // count, panels * (index + 1) // count):
        top = slice(8 * b, 8 * b + 8)
        panel = work[top, :]
        spread = [jnp.broadcast_to(panel[:, 8 * b + j : 8 * b + j + 1], (8, n)) for j in range(8)]
        e = [
            [jnp.broadcast_to(spread[j][i : i + 1, :], (8, n)) for j in range(i + 1)]
            for i in range(8)
        ]
        left = [jnp.broadcast_to(panel[i : i + 1, :n], (8, n)) for i in range(8)]
        right = [jnp.broadcast_to(panel[i : i + 1, n:], (8, n)) for i in range(8)]
        for j in range(8):
            scale = lax.rsqrt(e[j][j])
            left[j] = left[j] * scale
            right[j] = right[j] * scale
            low = {i: e[i][j] * scale for i in range(j + 1, 8)}
            for i in range(j + 1, 8):
                for k in range(j + 1, i + 1):
                    e[i][k] = e[i][k] - low[i] * low[k]
                left[i] = left[i] - low[i] * left[j]
                right[i] = right[i] - low[i] * right[j]
        l_panel, r_panel = left[0], right[0]
        for i in range(1, 8):
            l_panel = jnp.where(sub == i, left[i], l_panel)
            r_panel = jnp.where(sub == i, right[i], r_panel)
        work[top, n:] = r_panel
        if b < panels - 1:
            done = jnp.concatenate([l_panel, r_panel], 1)
            change = dot(l_panel, done, 0, 0)
            below = slice(8 * b + 8, n)
            work[below, :] = work[below, :] - change[8 * b + 8 :, :]
    if last:
        out_ref[...] = work[:, n:]


def factor(index, count, value):
    n = value.shape[0]
    last = index == count - 1
    return pl.pallas_call(
        functools.partial(factor_kernel, index, count),
        in_specs=[VMEM],
        out_specs=VMEM,
        out_shape=jax.ShapeDtypeStruct((n, n if last else 2 * n), f32),
        scratch_shapes=[pltpu.VMEM((n, 2 * n), f32)] if last else [],
        compiler_params=params(),
        cost_estimate=cost(0.01),
        name="factor",
    )(value)


def finish_kernel(orders, own_ref, inverse_ref, *refs):
    count = 2 * len(orders)
    parts, (out_ref, gram_ref, total) = refs[:count], refs[count:]
    for piece, places in enumerate(orders):
        keep, other = parts[2 * piece], parts[2 * piece + 1]
        half = len(places) // 2
        step = keep.shape[0] // half
        for i in range(half):
            for ref, place in ((keep, places[i]), (other, places[half + i])):
                at = piece * 2 * half * step + (place ^ own_ref[1]) * step
                total[pl.ds(pl.multiple_of(at, step), step)] = ref[i * step : (i + 1) * step]
    value = jnp.dot(inverse_ref[...], total[...], precision=full, preferred_element_type=f32)
    out_ref[...] = value
    gram_ref[...] = dot(value, value, 1, 1)


def finish(own, inverse, parts, orders):
    width = inverse.shape[0]
    cols = parts[0].shape[1]
    return pl.pallas_call(
        functools.partial(finish_kernel, orders),
        in_specs=[SMEM] + [VMEM] * (1 + len(parts)),
        out_specs=[VMEM] * 2,
        out_shape=[
            jax.ShapeDtypeStruct((width, cols), f32),
            jax.ShapeDtypeStruct((width, width), f32),
        ],
        scratch_shapes=[pltpu.VMEM((width, cols), f32)],
        compiler_params=params(),
        cost_estimate=cost(8),
        name="finish",
    )(own, inverse, *parts)


def per_device(data, omega):
    nrow, ncol = lax.axis_size("row"), lax.axis_size("col")
    quarter = data.shape[0] // ncol
    assert ncol == 4 and quarter == 2 * PIECE and nrow >= 8
    total_rows = data.shape[0] * nrow
    own = jnp.stack([lax.axis_index("col"), lax.axis_index("row") % 8]).astype(jnp.int32)
    bits = [1 << k for k in range(nrow.bit_length() - 1)]

    near = pltpu.with_memory_space_constraint(data, pltpu.VMEM)
    data = pltpu.with_memory_space_constraint(data, pltpu.HBM)

    part, wide = sketch(own, data, omega, [3], True)
    (pair,) = sketch(own, data, wide, [2])
    pair, wide = fence((pair + swap(part, "col", 1), wide))
    away = swap(pair, "col", 2)
    part, here = sketch(own, near, wide, [1, 0], near=True)
    part_a, part_b, away = fence((swap(part[:PIECE], "col", 1), swap(part[PIECE:], "col", 1), away))
    sketched = here + jnp.concatenate([part_a, part_b], 0) + away

    third = swap(sketched, "col", 2)
    second = swap(sketched, "col", 1)
    gram = dot(sketched, sketched, 0, 0)
    far = swap(gram, "row", bits[0])
    (acc,) = project(own, near, [0], [sketched])
    far, acc, second = fence((far, acc, second))
    gram = gram + far
    far = swap(gram, "row", bits[1])
    (acc,) = project(own, near, [1], [second], acc)
    far, acc = fence((far, acc))
    gram = gram + far
    for bit in bits[2:]:
        gram = gram + swap(gram, "row", bit)
    gram = gram + swap(gram, "col", 1)
    third, gram, acc = fence((third, gram, acc))
    fourth = swap(third, "col", 1)
    far = swap(gram, "col", 2)
    (acc,) = project(own, near, [2], [third], acc)
    far, acc, fourth = fence((far, acc, fourth))
    gram = gram + far
    cuts = [(1, 2, 4), (2, 4, 1)]
    orders = [order(cut) for cut in cuts]
    sums = project(own, near, [3], [fourth], acc, orders)

    *sums, state = fence((*sums, gram))
    sends, keeps = sums[0::2], sums[1::2]

    def exchange(values, step, beside):
        got = [swap(v, "row", cut[step]) for v, cut in zip(values, cuts)]
        *got, beside = fence((*got, beside))
        return got, beside

    for k in range(3):
        got, state = exchange(sends, k, factor(k, 4, state))
        keeps = [v + w for v, w in zip(keeps, got)]
        if k < 2:
            half = keeps[0].shape[0] // 2
            *cut_up, state = fence((*[v[half:] for v in keeps], *[v[:half] for v in keeps], state))
            sends, keeps = cut_up[:2], cut_up[2:]
    for bit in bits[3:]:
        keeps = [v + swap(v, "row", bit) for v in keeps]
    *keeps, state = fence((*keeps, state))
    got, inverse = exchange(keeps, 2, factor(3, 4, state))
    keeps = [jnp.concatenate([v, w], 0) for v, w in zip(keeps, got)]
    *keeps, inverse = fence((*keeps, inverse))
    got, basis = exchange(keeps, 1, dot(sketched, inverse, 1, 1))
    keeps = [jnp.concatenate([v, w], 0) for v, w in zip(keeps, got)]
    *keeps, basis = fence((*keeps, basis))
    parts = []
    for v, cut in zip(keeps, cuts):
        parts += [v, swap(v, "row", cut[0])]

    projected, small = finish(own, inverse, parts, orders)
    across = [swap(small, "col", bit) for bit in (2, 3, 1)]
    small = (small + across[2]) + (across[0] + across[1])
    return (basis, projected, small / total_rows)


def solution(mesh):
    placed = (P("row", "col"), P("col", None))
    return jax.shard_map(
        per_device,
        mesh=mesh,
        in_specs=placed,
        out_specs=(P(("row", "col"), None), P(None, "col"), P()),
        check_vma=False,
    )
```

```python
import functools

import jax
import jax.numpy as jnp
from jax import lax
from jax.experimental import pallas as pl
from jax.experimental.pallas import tpu as pltpu
from jax.sharding import PartitionSpec as P

full = lax.Precision.HIGHEST
f32 = jnp.float32
bf16 = jnp.bfloat16

PIECE = 512
TILE = 256
SMEM = pl.BlockSpec(memory_space=pltpu.SMEM)
VMEM = pl.BlockSpec(memory_space=pltpu.VMEM)
HBM = pl.BlockSpec(memory_space=pltpu.HBM)
fence = lax.optimization_barrier


def cost(mib):
    return pl.CostEstimate(flops=1, bytes_accessed=int(mib * 2**20), transcendentals=0)


def params():
    return pltpu.CompilerParams(vmem_limit_bytes=16 * 1024 * 1024)


def swap(value, axis, bit):
    return lax.ppermute(value, axis, [(i, i ^ bit) for i in range(lax.axis_size(axis))])


def dot(a, b, a_dim, b_dim, precision=full):
    return lax.dot_general(
        a, b, (((a_dim,), (b_dim,)), ((), ())), precision=precision, preferred_element_type=f32
    )


def split(value):
    upper = value.astype(bf16)
    return upper, (value - upper.astype(f32)).astype(bf16)


def sketch_kernel(places, first, own_ref, data_ref, omega_ref, *refs):
    count = len(places)
    if first:
        refs, (omega_held, omega_sem) = refs[:-2], refs[-2:]
        omega_copy = pltpu.make_async_copy(omega_ref, omega_held, omega_sem)
        omega_copy.start()
    outs, held, sems = refs[:count], refs[count : 2 * count], refs[-1]
    quarter, cols = held[0].shape
    copies = {}
    for k, place in enumerate(places):
        for row in range(0, quarter, PIECE):
            at = pl.multiple_of((own_ref[0] ^ place) * quarter + row, PIECE)
            for t in range(cols // TILE):
                tile = pl.ds(t * TILE, TILE)
                copy = pltpu.make_async_copy(
                    data_ref.at[pl.ds(at, PIECE), tile],
                    held[k].at[pl.ds(row, PIECE), tile],
                    sems.at[k, row // PIECE, t],
                )
                copy.start()
                copies[k, row, t] = copy
    if first:
        width = omega_ref.shape[1]
        wide = refs[2 * count]
        omega_copy.wait()
        upper, rest = split(omega_held[...])
        wide[:, :width] = upper
        wide[:, width:] = rest
    else:
        wide = omega_ref
        width = omega_ref.shape[1] // 2
    for (k, row, t), copy in copies.items():
        tile = slice(t * TILE, (t + 1) * TILE)
        copy.wait()
        upper, rest = split(held[k][row : row + PIECE, tile])
        one = jnp.dot(upper, wide[tile, :], preferred_element_type=f32)
        two = jnp.dot(rest, wide[tile, :width], preferred_element_type=f32)
        both, more = (one, two) if t == 0 else (both + one, more + two)
        if t == cols // TILE - 1:
            outs[k][row : row + PIECE] = both[:, :width] + both[:, width:] + more


def sketch(own, data, omega, places, first=False):
    cols = data.shape[1]
    width = omega.shape[1] if first else omega.shape[1] // 2
    quarter = data.shape[0] // lax.axis_size("col")
    count = len(places)
    out = [jax.ShapeDtypeStruct((quarter, width), f32)] * count
    out += [pltpu.VMEM((quarter, cols), f32)] * count
    scratch = [pltpu.SemaphoreType.DMA((count, quarter // PIECE, cols // TILE))]
    if first:
        out.append(jax.ShapeDtypeStruct((cols, 2 * width), bf16))
        scratch += [pltpu.VMEM(omega.shape, f32), pltpu.SemaphoreType.DMA]
    return pl.pallas_call(
        functools.partial(sketch_kernel, places, first),
        in_specs=[SMEM, HBM, HBM if first else VMEM],
        out_specs=[VMEM] * len(out),
        out_shape=out,
        scratch_shapes=scratch,
        compiler_params=params(),
        cost_estimate=cost(0.01),
        name="partial_sketch",
    )(own, data, omega)


def project_kernel(before, slices, own_ref, rows_ref, part_ref, *refs):
    old, refs = (refs[0], refs[1:]) if before else (None, refs)
    outs, total = (refs[:-1], refs[-1]) if slices else (refs, refs[0])
    quarter, cols = rows_ref.shape
    for row in range(0, quarter, PIECE):
        upper, rest = split(part_ref[row : row + PIECE].T)
        stack = jnp.concatenate([upper, rest], 0)
        width = upper.shape[0]
        for t in range(cols // TILE):
            tile = slice(t * TILE, (t + 1) * TILE)
            d_upper, d_rest = split(rows_ref[row : row + PIECE, tile])
            both = jnp.dot(stack, d_upper, preferred_element_type=f32)
            value = both[:width] + both[width:] + jnp.dot(upper, d_rest, preferred_element_type=f32)
            if row > 0:
                value += total[:, tile]
            elif before:
                value += old[:, tile]
            total[:, tile] = value
    if slices:
        step = outs[0].shape[0]
        for place, ref in enumerate(outs):
            at = pl.multiple_of((place ^ own_ref[1]) * step, step)
            ref[...] = total[pl.ds(at, step)]


def project(own, rows, part, before=None, slices=0):
    cols = rows.shape[1]
    width = part.shape[1]
    args = [own, rows, part] + ([] if before is None else [before])
    if slices:
        out = [jax.ShapeDtypeStruct((width // slices, cols), f32)] * slices
    else:
        out = [jax.ShapeDtypeStruct((width, cols), f32)]
    return pl.pallas_call(
        functools.partial(project_kernel, before is not None, slices),
        in_specs=[SMEM] + [VMEM] * (len(args) - 1),
        out_specs=[VMEM] * len(out),
        out_shape=out,
        scratch_shapes=[pltpu.VMEM((width, cols), f32)] if slices else [],
        compiler_params=params(),
        cost_estimate=cost(6),
        name="project",
    )(*args)


def factor_kernel(index, count, in_ref, out_ref, *scratch):
    n = in_ref.shape[0]
    last = index == count - 1
    work = scratch[0] if last else out_ref
    if index == 0:
        row = lax.broadcasted_iota(jnp.int32, (n, n), 0)
        col = lax.broadcasted_iota(jnp.int32, (n, n), 1)
        work[:, :n] = in_ref[...]
        work[:, n:] = jnp.where(row == col, 1.0, 0.0).astype(f32)
    else:
        work[...] = in_ref[...]
    sub = lax.broadcasted_iota(jnp.int32, (8, n), 0)
    panels = n // 8
    for b in range(panels * index // count, panels * (index + 1) // count):
        top = slice(8 * b, 8 * b + 8)
        panel = work[top, :]
        spread = [jnp.broadcast_to(panel[:, 8 * b + j : 8 * b + j + 1], (8, n)) for j in range(8)]
        e = [
            [jnp.broadcast_to(spread[j][i : i + 1, :], (8, n)) for j in range(i + 1)]
            for i in range(8)
        ]
        left = [jnp.broadcast_to(panel[i : i + 1, :n], (8, n)) for i in range(8)]
        right = [jnp.broadcast_to(panel[i : i + 1, n:], (8, n)) for i in range(8)]
        for j in range(8):
            scale = lax.rsqrt(e[j][j])
            left[j] = left[j] * scale
            right[j] = right[j] * scale
            low = {i: e[i][j] * scale for i in range(j + 1, 8)}
            for i in range(j + 1, 8):
                for k in range(j + 1, i + 1):
                    e[i][k] = e[i][k] - low[i] * low[k]
                left[i] = left[i] - low[i] * left[j]
                right[i] = right[i] - low[i] * right[j]
        l_panel, r_panel = left[0], right[0]
        for i in range(1, 8):
            l_panel = jnp.where(sub == i, left[i], l_panel)
            r_panel = jnp.where(sub == i, right[i], r_panel)
        work[top, n:] = r_panel
        if b < panels - 1:
            done = jnp.concatenate([l_panel, r_panel], 1)
            change = dot(l_panel, done, 0, 0)
            below = slice(8 * b + 8, n)
            work[below, :] = work[below, :] - change[8 * b + 8 :, :]
    if last:
        out_ref[...] = work[:, n:]


def factor(index, count, value):
    n = value.shape[0]
    last = index == count - 1
    return pl.pallas_call(
        functools.partial(factor_kernel, index, count),
        in_specs=[VMEM],
        out_specs=VMEM,
        out_shape=jax.ShapeDtypeStruct((n, n if last else 2 * n), f32),
        scratch_shapes=[pltpu.VMEM((n, 2 * n), f32)] if last else [],
        compiler_params=params(),
        cost_estimate=cost(0.01),
        name="factor",
    )(value)


def finish_kernel(own_ref, inverse_ref, *refs):
    parts, (out_ref, gram_ref, total) = refs[:-3], refs[-3:]
    step = parts[0].shape[0]
    for place, ref in enumerate(parts):
        at = pl.multiple_of((place ^ own_ref[1]) * step, step)
        total[pl.ds(at, step)] = ref[...]
    value = jnp.dot(inverse_ref[...], total[...], precision=full, preferred_element_type=f32)
    out_ref[...] = value
    gram_ref[...] = dot(value, value, 1, 1)


def finish(own, inverse, parts):
    width = inverse.shape[0]
    cols = parts[0].shape[1]
    return pl.pallas_call(
        finish_kernel,
        in_specs=[SMEM] + [VMEM] * (1 + len(parts)),
        out_specs=[VMEM] * 2,
        out_shape=[
            jax.ShapeDtypeStruct((width, cols), f32),
            jax.ShapeDtypeStruct((width, width), f32),
        ],
        scratch_shapes=[pltpu.VMEM((width, cols), f32)],
        compiler_params=params(),
        cost_estimate=cost(8),
        name="finish",
    )(own, inverse, *parts)


def per_device(data, omega):
    nrow, ncol = lax.axis_size("row"), lax.axis_size("col")
    quarter = data.shape[0] // ncol
    assert ncol == 4 and quarter == 2 * PIECE and nrow >= 8
    total_rows = data.shape[0] * nrow
    own = jnp.stack([lax.axis_index("col"), lax.axis_index("row") % 8]).astype(jnp.int32)
    bits = [1 << k for k in range(nrow.bit_length() - 1)]

    data = pltpu.with_memory_space_constraint(data, pltpu.HBM)
    omega = pltpu.with_memory_space_constraint(omega, pltpu.HBM)

    part, rows3, wide = sketch(own, data, omega, [3], True)
    pair, rows2 = sketch(own, data, wide, [2])
    pair, wide = fence((pair + swap(part, "col", 1), wide))
    away = swap(pair, "col", 2)
    part, here, rows1, rows0 = sketch(own, data, wide, [1, 0])
    part_a, part_b, away = fence((swap(part[:PIECE], "col", 1), swap(part[PIECE:], "col", 1), away))
    sketched = here + jnp.concatenate([part_a, part_b], 0) + away

    third = swap(sketched, "col", 2)
    second = swap(sketched, "col", 1)
    gram = dot(sketched, sketched, 0, 0)
    far = swap(gram, "row", bits[0])
    (acc,) = project(own, rows0, sketched)
    far, acc, second = fence((far, acc, second))
    gram = gram + far
    far = swap(gram, "row", bits[1])
    (acc,) = project(own, rows1, second, acc)
    far, acc = fence((far, acc))
    gram = gram + far
    far = swap(gram, "row", bits[2])
    third, acc = fence((third, acc))
    fourth = swap(third, "col", 1)
    (acc,) = project(own, rows2, third, acc)
    far, acc, fourth = fence((far, acc, fourth))
    gram = gram + far
    for bit in bits[3:]:
        gram = gram + swap(gram, "row", bit)
    far = swap(gram, "col", 1)
    slices = project(own, rows3, fourth, acc, 8)
    far, *slices = fence((far, *slices))
    gram = gram + far

    state = factor(0, 2, gram + swap(gram, "col", 2))
    got = [swap(slices[q], "row", q) for q in range(1, 8)]
    *got, state = fence((*got, state))
    mine = ((slices[0] + got[0]) + (got[1] + got[2])) + ((got[3] + got[4]) + (got[5] + got[6]))
    for bit in bits[3:]:
        mine = mine + swap(mine, "row", bit)
    mine, state = fence((mine, state))
    inverse = factor(1, 2, state)
    got = [swap(mine, "row", q) for q in range(1, 8)]
    *got, inverse = fence((*got, inverse))
    projected, small = finish(own, inverse, [mine, *got])

    across = [swap(small, "col", bit) for bit in (2, 3, 1)]
    *across, basis = fence((*across, dot(sketched, inverse, 1, 1)))
    small = (small + across[2]) + (across[0] + across[1])
    return (basis, projected, small / total_rows)


def solution(mesh):
    placed = (P("row", "col"), P("col", None))
    return jax.shard_map(
        per_device,
        mesh=mesh,
        in_specs=placed,
        out_specs=(P(("row", "col"), None), P(None, "col"), P()),
        check_vma=False,
    )
```

```python
import functools

import jax
import jax.numpy as jnp
from jax import lax
from jax.experimental import pallas as pl
from jax.experimental.pallas import tpu as pltpu
from jax.sharding import PartitionSpec as P

full = lax.Precision.HIGHEST
f32 = jnp.float32
bf16 = jnp.bfloat16

PIECE = 512
TILE = 256
RUN = 128
SLICES = 8
SMEM = pl.BlockSpec(memory_space=pltpu.SMEM)
VMEM = pl.BlockSpec(memory_space=pltpu.VMEM)
HBM = pl.BlockSpec(memory_space=pltpu.HBM)
fence = lax.optimization_barrier


def cost(mib):
    return pl.CostEstimate(flops=1, bytes_accessed=int(mib * 2**20), transcendentals=0)


def params():
    return pltpu.CompilerParams(vmem_limit_bytes=16 * 1024 * 1024)


def swap(value, axis, bit):
    return lax.ppermute(value, axis, [(i, i ^ bit) for i in range(lax.axis_size(axis))])


def dot(a, b, a_dim, b_dim, precision=full):
    return lax.dot_general(
        a, b, (((a_dim,), (b_dim,)), ((), ())), precision=precision, preferred_element_type=f32
    )


def split(value):
    upper = value.astype(bf16)
    return upper, (value - upper.astype(f32)).astype(bf16)


def sketch_kernel(places, first, own_ref, data_ref, omega_ref, *refs):
    count = len(places)
    if first:
        refs, (omega_held, omega_sem) = refs[:-2], refs[-2:]
        omega_copy = pltpu.make_async_copy(omega_ref, omega_held, omega_sem)
        omega_copy.start()
    outs, held, sems = refs[:count], refs[count : 2 * count], refs[-1]
    quarter, cols = held[0].shape
    copies = {}
    for k, place in enumerate(places):
        for row in range(0, quarter, RUN):
            at = pl.multiple_of((own_ref[0] ^ place) * quarter + row, RUN)
            copy = pltpu.make_async_copy(
                data_ref.at[pl.ds(at, RUN)], held[k].at[pl.ds(row, RUN)], sems.at[k, row // RUN]
            )
            copy.start()
            copies[k, row] = copy
    if first:
        width = omega_ref.shape[1]
        wide = refs[2 * count]
        omega_copy.wait()
        upper, rest = split(omega_held[...])
        wide[:, :width] = upper
        wide[:, width:] = rest
    else:
        wide = omega_ref
        width = omega_ref.shape[1] // 2
    for k in range(count):
        for row in range(0, quarter, PIECE):
            for run in range(row, row + PIECE, RUN):
                copies[k, run].wait()
            for t in range(cols // TILE):
                tile = slice(t * TILE, (t + 1) * TILE)
                upper, rest = split(held[k][row : row + PIECE, tile])
                one = jnp.dot(upper, wide[tile, :], preferred_element_type=f32)
                two = jnp.dot(rest, wide[tile, :width], preferred_element_type=f32)
                both, more = (one, two) if t == 0 else (both + one, more + two)
            outs[k][row : row + PIECE] = both[:, :width] + both[:, width:] + more


def sketch(own, data, omega, places, first=False):
    cols = data.shape[1]
    width = omega.shape[1] if first else omega.shape[1] // 2
    quarter = data.shape[0] // lax.axis_size("col")
    count = len(places)
    out = [jax.ShapeDtypeStruct((quarter, width), f32)] * count
    out += [pltpu.VMEM((quarter, cols), f32)] * count
    scratch = [pltpu.SemaphoreType.DMA((count, quarter // RUN))]
    if first:
        out.append(jax.ShapeDtypeStruct((cols, 2 * width), bf16))
        scratch += [pltpu.VMEM(omega.shape, f32), pltpu.SemaphoreType.DMA]
    return pl.pallas_call(
        functools.partial(sketch_kernel, places, first),
        in_specs=[SMEM, HBM, HBM if first else VMEM],
        out_specs=[VMEM] * len(out),
        out_shape=out,
        scratch_shapes=scratch,
        compiler_params=params(),
        cost_estimate=cost(0.01),
        name="partial_sketch",
    )(own, data, omega)


def project_kernel(before, slices, own_ref, rows_ref, part_ref, *refs):
    old, refs = (refs[0], refs[1:]) if before else (None, refs)
    outs, total = (refs[:-1], refs[-1]) if slices else (refs, refs[0])
    quarter, cols = rows_ref.shape
    for row in range(0, quarter, PIECE):
        upper, rest = split(part_ref[row : row + PIECE].T)
        stack = jnp.concatenate([upper, rest], 0)
        width = upper.shape[0]
        for t in range(cols // TILE):
            tile = slice(t * TILE, (t + 1) * TILE)
            d_upper, d_rest = split(rows_ref[row : row + PIECE, tile])
            both = jnp.dot(stack, d_upper, preferred_element_type=f32)
            value = both[:width] + both[width:] + jnp.dot(upper, d_rest, preferred_element_type=f32)
            if row > 0:
                value += total[:, tile]
            elif before:
                value += old[:, tile]
            total[:, tile] = value
    if slices:
        step = total.shape[0] // slices
        for place in range(slices):
            at = pl.multiple_of((place ^ own_ref[1]) * step, step)
            row = place // 2 * step
            outs[1 - place % 2][row : row + step] = total[pl.ds(at, step)]


def project(own, rows, part, before=None, slices=0):
    cols = rows.shape[1]
    width = part.shape[1]
    args = [own, rows, part] + ([] if before is None else [before])
    if slices:
        out = [jax.ShapeDtypeStruct((width // 2, cols), f32)] * 2
    else:
        out = [jax.ShapeDtypeStruct((width, cols), f32)]
    return pl.pallas_call(
        functools.partial(project_kernel, before is not None, slices),
        in_specs=[SMEM] + [VMEM] * (len(args) - 1),
        out_specs=[VMEM] * len(out),
        out_shape=out,
        scratch_shapes=[pltpu.VMEM((width, cols), f32)] if slices else [],
        compiler_params=params(),
        cost_estimate=cost(6),
        name="project",
    )(*args)


def factor_kernel(index, count, in_ref, out_ref, *scratch):
    n = in_ref.shape[0]
    last = index == count - 1
    work = scratch[0] if last else out_ref
    if index == 0:
        row = lax.broadcasted_iota(jnp.int32, (n, n), 0)
        col = lax.broadcasted_iota(jnp.int32, (n, n), 1)
        work[:, :n] = in_ref[...]
        work[:, n:] = jnp.where(row == col, 1.0, 0.0).astype(f32)
    else:
        work[...] = in_ref[...]
    sub = lax.broadcasted_iota(jnp.int32, (8, n), 0)
    panels = n // 8
    for b in range(panels * index // count, panels * (index + 1) // count):
        top = slice(8 * b, 8 * b + 8)
        panel = work[top, :]
        spread = [jnp.broadcast_to(panel[:, 8 * b + j : 8 * b + j + 1], (8, n)) for j in range(8)]
        e = [
            [jnp.broadcast_to(spread[j][i : i + 1, :], (8, n)) for j in range(i + 1)]
            for i in range(8)
        ]
        left = [jnp.broadcast_to(panel[i : i + 1, :n], (8, n)) for i in range(8)]
        right = [jnp.broadcast_to(panel[i : i + 1, n:], (8, n)) for i in range(8)]
        for j in range(8):
            scale = lax.rsqrt(e[j][j])
            left[j] = left[j] * scale
            right[j] = right[j] * scale
            low = {i: e[i][j] * scale for i in range(j + 1, 8)}
            for i in range(j + 1, 8):
                for k in range(j + 1, i + 1):
                    e[i][k] = e[i][k] - low[i] * low[k]
                left[i] = left[i] - low[i] * left[j]
                right[i] = right[i] - low[i] * right[j]
        l_panel, r_panel = left[0], right[0]
        for i in range(1, 8):
            l_panel = jnp.where(sub == i, left[i], l_panel)
            r_panel = jnp.where(sub == i, right[i], r_panel)
        work[top, n:] = r_panel
        if b < panels - 1:
            rows = slice(8 * b + 8, 8 * b + 16)
            l_next, r_next = work[rows, :n], work[rows, n:]
            column = l_panel.T[rows, :]
            for j in range(8):
                factors = jnp.broadcast_to(column[:, j : j + 1], (8, n))
                l_next = l_next - factors * left[j]
                r_next = r_next - factors * right[j]
            work[rows, :n] = l_next
            work[rows, n:] = r_next
        if b < panels - 2:
            done = jnp.concatenate([l_panel, r_panel], 1)
            change = dot(l_panel, done, 0, 0)
            below = slice(8 * b + 16, n)
            work[below, :] = work[below, :] - change[8 * b + 16 :, :]
    if last:
        out_ref[...] = work[:, n:]


def factor(index, count, value):
    n = value.shape[0]
    last = index == count - 1
    return pl.pallas_call(
        functools.partial(factor_kernel, index, count),
        in_specs=[VMEM],
        out_specs=VMEM,
        out_shape=jax.ShapeDtypeStruct((n, n if last else 2 * n), f32),
        scratch_shapes=[pltpu.VMEM((n, 2 * n), f32)] if last else [],
        compiler_params=params(),
        cost_estimate=cost(0.01),
        name="factor",
    )(value)


def finish_kernel(own_ref, inverse_ref, *refs):
    parts, (out_ref, gram_ref, total) = refs[:-3], refs[-3:]
    step = total.shape[0] // SLICES
    for place in range(SLICES):
        at = pl.multiple_of((place ^ own_ref[1]) * step, step)
        row = place // 2 * step
        total[pl.ds(at, step)] = parts[place % 2][row : row + step]
    value = jnp.dot(inverse_ref[...], total[...], precision=full, preferred_element_type=f32)
    out_ref[...] = value
    gram_ref[...] = dot(value, value, 1, 1)


def finish(own, inverse, parts):
    width = inverse.shape[0]
    cols = parts[0].shape[1]
    return pl.pallas_call(
        finish_kernel,
        in_specs=[SMEM] + [VMEM] * (1 + len(parts)),
        out_specs=[VMEM] * 2,
        out_shape=[
            jax.ShapeDtypeStruct((width, cols), f32),
            jax.ShapeDtypeStruct((width, width), f32),
        ],
        scratch_shapes=[pltpu.VMEM((width, cols), f32)],
        compiler_params=params(),
        cost_estimate=cost(8),
        name="finish",
    )(own, inverse, *parts)


def per_device(data, omega):
    nrow, ncol = lax.axis_size("row"), lax.axis_size("col")
    quarter = data.shape[0] // ncol
    assert ncol == 4 and quarter == 2 * PIECE and nrow >= 8
    total_rows = data.shape[0] * nrow
    own = jnp.stack([lax.axis_index("col"), lax.axis_index("row") % 8]).astype(jnp.int32)
    bits = [1 << k for k in range(nrow.bit_length() - 1)]

    data = pltpu.with_memory_space_constraint(data, pltpu.HBM)
    omega = pltpu.with_memory_space_constraint(omega, pltpu.HBM)

    part, rows3, wide = sketch(own, data, omega, [3], True)
    pair, rows2 = sketch(own, data, wide, [2])
    pair, wide = fence((pair + swap(part, "col", 1), wide))
    away = swap(pair, "col", 2)
    part, here, rows1, rows0 = sketch(own, data, wide, [1, 0])
    part_a, part_b, away = fence((swap(part[:PIECE], "col", 1), swap(part[PIECE:], "col", 1), away))
    sketched = here + jnp.concatenate([part_a, part_b], 0) + away

    third = swap(sketched, "col", 2)
    second = swap(sketched, "col", 1)
    gram = dot(sketched, sketched, 0, 0)
    far = swap(gram, "row", bits[0])
    (acc,) = project(own, rows0, sketched)
    far, acc, second = fence((far, acc, second))
    gram = gram + far
    far = swap(gram, "row", bits[1])
    (acc,) = project(own, rows1, second, acc)
    far, acc = fence((far, acc))
    gram = gram + far
    far = swap(gram, "row", bits[2])
    third, acc, far = fence((third, acc, far))
    fourth = swap(third, "col", 1)
    (acc,) = project(own, rows2, third, acc)
    acc, fourth = fence((acc, fourth))
    gram = gram + far
    for bit in bits[3:]:
        gram = gram + swap(gram, "row", bit)
    far = swap(gram, "col", 1)
    send, keep = project(own, rows3, fourth, acc, SLICES)
    far, send, keep = fence((far, send, keep))
    gram = gram + far

    got, state = fence((swap(send, "row", 1), factor(0, 3, gram + swap(gram, "col", 2))))
    step = keep.shape[0] // 4
    quads = [keep[i * step : (i + 1) * step] + got[i * step : (i + 1) * step] for i in range(4)]
    *quads, state = fence((*quads, state))
    got = [swap(quads[i], "row", 2 * i) for i in (1, 2, 3)]
    *got, state = fence((*got, factor(1, 3, state)))
    mine = (quads[0] + got[0]) + (got[1] + got[2])
    for bit in bits[3:]:
        mine = mine + swap(mine, "row", bit)
    mine, state = fence((mine, state))
    got = [swap(mine, "row", 2 * i) for i in (1, 2, 3)]
    *got, inverse = fence((*got, factor(2, 3, state)))
    keep = jnp.concatenate([mine, *got], 0)
    keep, inverse = fence((keep, inverse))
    got, basis = fence((swap(keep, "row", 1), dot(sketched, inverse, 1, 1)))
    projected, small = finish(own, inverse, [keep, got])

    across = [swap(small, "col", bit) for bit in (2, 3, 1)]
    small = (small + across[2]) + (across[0] + across[1])
    return (basis, projected, small / total_rows)


def solution(mesh):
    placed = (P("row", "col"), P("col", None))
    return jax.shard_map(
        per_device,
        mesh=mesh,
        in_specs=placed,
        out_specs=(P(("row", "col"), None), P(None, "col"), P()),
        check_vma=False,
    )
```

```python
import functools

import jax
import jax.numpy as jnp
from jax import lax
from jax.experimental import pallas as pl
from jax.experimental.pallas import tpu as pltpu
from jax.sharding import PartitionSpec as P

full = lax.Precision.HIGHEST
f32 = jnp.float32
bf16 = jnp.bfloat16

PIECE = 512
TILE = 256
RUN = 128
SLICES = 8
SMEM = pl.BlockSpec(memory_space=pltpu.SMEM)
VMEM = pl.BlockSpec(memory_space=pltpu.VMEM)
HBM = pl.BlockSpec(memory_space=pltpu.HBM)
fence = lax.optimization_barrier


def cost(mib):
    return pl.CostEstimate(flops=1, bytes_accessed=int(mib * 2**20), transcendentals=0)


def params():
    return pltpu.CompilerParams(vmem_limit_bytes=16 * 1024 * 1024)


def swap(value, axis, bit):
    return lax.ppermute(value, axis, [(i, i ^ bit) for i in range(lax.axis_size(axis))])


def dot(a, b, a_dim, b_dim, precision=full):
    return lax.dot_general(
        a, b, (((a_dim,), (b_dim,)), ((), ())), precision=precision, preferred_element_type=f32
    )


def split(value):
    upper = value.astype(bf16)
    return upper, (value - upper.astype(f32)).astype(bf16)


def multiply(held, wide, out):
    quarter, cols = held.shape
    width = out.shape[1]
    for row in range(0, quarter, PIECE):
        yield row
        for t in range(cols // TILE):
            tile = slice(t * TILE, (t + 1) * TILE)
            upper, rest = split(held[row : row + PIECE, tile])
            one = jnp.dot(upper, wide[tile, :], preferred_element_type=f32)
            two = jnp.dot(rest, wide[tile, :width], preferred_element_type=f32)
            both, more = (one, two) if t == 0 else (both + one, more + two)
        out[row : row + PIECE] = both[:, :width] + both[:, width:] + more


def sketch_kernel(places, ahead, first, own_ref, data_ref, omega_ref, *refs):
    count, total = len(places), len(places) + len(ahead)
    if first:
        refs, (omega_held, omega_sem) = refs[:-2], refs[-2:]
        omega_copy = pltpu.make_async_copy(omega_ref, omega_held, omega_sem)
        omega_copy.start()
    outs, held, sems = refs[:count], refs[count : count + total], refs[-1]
    quarter = held[0].shape[0]
    copies = {}
    for k, place in enumerate(places + ahead):
        for row in range(0, quarter, RUN):
            at = pl.multiple_of((own_ref[0] ^ place) * quarter + row, RUN)
            copy = pltpu.make_async_copy(
                data_ref.at[pl.ds(at, RUN)], held[k].at[pl.ds(row, RUN)], sems.at[k, row // RUN]
            )
            copy.start()
            copies[k, row] = copy
    if first:
        width = omega_ref.shape[1]
        wide = refs[count + total]
        omega_copy.wait()
        upper, rest = split(omega_held[...])
        wide[:, :width] = upper
        wide[:, width:] = rest
    else:
        wide = omega_ref
    for k in range(count):
        for row in multiply(held[k], wide, outs[k]):
            for run in range(row, row + PIECE, RUN):
                copies[k, run].wait()
    for k in range(count, total):
        for row in range(0, quarter, RUN):
            copies[k, row].wait()


def sketch(own, data, omega, places, ahead=(), first=False):
    cols = data.shape[1]
    width = omega.shape[1] if first else omega.shape[1] // 2
    quarter = data.shape[0] // lax.axis_size("col")
    total = len(places) + len(ahead)
    out = [jax.ShapeDtypeStruct((quarter, width), f32)] * len(places)
    out += [pltpu.VMEM((quarter, cols), f32)] * total
    scratch = [pltpu.SemaphoreType.DMA((total, quarter // RUN))]
    if first:
        out.append(jax.ShapeDtypeStruct((cols, 2 * width), bf16))
        scratch += [pltpu.VMEM(omega.shape, f32), pltpu.SemaphoreType.DMA]
    return pl.pallas_call(
        functools.partial(sketch_kernel, places, ahead, first),
        in_specs=[SMEM, HBM, HBM if first else VMEM],
        out_specs=[VMEM] * len(out),
        out_shape=out,
        scratch_shapes=scratch,
        compiler_params=params(),
        cost_estimate=cost(0.01),
        name="partial_sketch",
    )(own, data, omega)


def held_kernel(rows_ref, wide_ref, out_ref):
    for _ in multiply(rows_ref, wide_ref, out_ref):
        pass


def sketch_held(rows, wide):
    return pl.pallas_call(
        held_kernel,
        in_specs=[VMEM] * 2,
        out_specs=VMEM,
        out_shape=jax.ShapeDtypeStruct((rows.shape[0], wide.shape[1] // 2), f32),
        compiler_params=params(),
        cost_estimate=cost(0.01),
        name="partial_sketch_held",
    )(rows, wide)


def project_kernel(start, before, slices, own_ref, rows_ref, part_ref, *refs):
    old, refs = (refs[0], refs[1:]) if before else (None, refs)
    outs, total = (refs[:-1], refs[-1]) if slices else (refs, refs[0])
    cols = rows_ref.shape[1]
    for row in range(0, part_ref.shape[0], PIECE):
        upper, rest = split(part_ref[row : row + PIECE].T)
        stack = jnp.concatenate([upper, rest], 0)
        width = upper.shape[0]
        for t in range(cols // TILE):
            tile = slice(t * TILE, (t + 1) * TILE)
            d_upper, d_rest = split(rows_ref[start + row : start + row + PIECE, tile])
            both = jnp.dot(stack, d_upper, preferred_element_type=f32)
            value = both[:width] + both[width:] + jnp.dot(upper, d_rest, preferred_element_type=f32)
            if row > 0:
                value += total[:, tile]
            elif before:
                value += old[:, tile]
            total[:, tile] = value
    if slices:
        step = total.shape[0] // slices
        for place in range(slices):
            at = pl.multiple_of((place ^ own_ref[1]) * step, step)
            row = place // 2 * step
            outs[1 - place % 2][row : row + step] = total[pl.ds(at, step)]


def project(own, rows, part, before=None, slices=0, start=0):
    cols = rows.shape[1]
    width = part.shape[1]
    args = [own, rows, part] + ([] if before is None else [before])
    if slices:
        out = [jax.ShapeDtypeStruct((width // 2, cols), f32)] * 2
    else:
        out = [jax.ShapeDtypeStruct((width, cols), f32)]
    return pl.pallas_call(
        functools.partial(project_kernel, start, before is not None, slices),
        in_specs=[SMEM] + [VMEM] * (len(args) - 1),
        out_specs=[VMEM] * len(out),
        out_shape=out,
        scratch_shapes=[pltpu.VMEM((width, cols), f32)] if slices else [],
        compiler_params=params(),
        cost_estimate=cost(6 * part.shape[0] / rows.shape[0]),
        name="project",
    )(*args)


def factor_kernel(index, count, in_ref, out_ref, *scratch):
    n = in_ref.shape[0]
    last = index == count - 1
    work = scratch[0] if last else out_ref
    if index == 0:
        row = lax.broadcasted_iota(jnp.int32, (n, n), 0)
        col = lax.broadcasted_iota(jnp.int32, (n, n), 1)
        work[:, :n] = in_ref[...]
        work[:, n:] = jnp.where(row == col, 1.0, 0.0).astype(f32)
    else:
        work[...] = in_ref[...]
    sub = lax.broadcasted_iota(jnp.int32, (8, n), 0)
    panels = n // 8
    for b in range(panels * index // count, panels * (index + 1) // count):
        top = slice(8 * b, 8 * b + 8)
        panel = work[top, :]
        spread = [jnp.broadcast_to(panel[:, 8 * b + j : 8 * b + j + 1], (8, n)) for j in range(8)]
        e = [
            [jnp.broadcast_to(spread[j][i : i + 1, :], (8, n)) for j in range(i + 1)]
            for i in range(8)
        ]
        left = [jnp.broadcast_to(panel[i : i + 1, :n], (8, n)) for i in range(8)]
        right = [jnp.broadcast_to(panel[i : i + 1, n:], (8, n)) for i in range(8)]
        for j in range(8):
            scale = lax.rsqrt(e[j][j])
            left[j] = left[j] * scale
            right[j] = right[j] * scale
            low = {i: e[i][j] * scale for i in range(j + 1, 8)}
            for i in range(j + 1, 8):
                for k in range(j + 1, i + 1):
                    e[i][k] = e[i][k] - low[i] * low[k]
                left[i] = left[i] - low[i] * left[j]
                right[i] = right[i] - low[i] * right[j]
        l_panel, r_panel = left[0], right[0]
        for i in range(1, 8):
            l_panel = jnp.where(sub == i, left[i], l_panel)
            r_panel = jnp.where(sub == i, right[i], r_panel)
        work[top, n:] = r_panel
        if b < panels - 1:
            rows = slice(8 * b + 8, 8 * b + 16)
            l_next, r_next = work[rows, :n], work[rows, n:]
            column = l_panel.T[rows, :]
            for j in range(8):
                factors = jnp.broadcast_to(column[:, j : j + 1], (8, n))
                l_next = l_next - factors * left[j]
                r_next = r_next - factors * right[j]
            work[rows, :n] = l_next
            work[rows, n:] = r_next
        if b < panels - 2:
            done = jnp.concatenate([l_panel, r_panel], 1)
            change = dot(l_panel, done, 0, 0)
            below = slice(8 * b + 16, n)
            work[below, :] = work[below, :] - change[8 * b + 16 :, :]
    if last:
        out_ref[...] = work[:, n:]


def factor(index, count, value):
    n = value.shape[0]
    last = index == count - 1
    return pl.pallas_call(
        functools.partial(factor_kernel, index, count),
        in_specs=[VMEM],
        out_specs=VMEM,
        out_shape=jax.ShapeDtypeStruct((n, n if last else 2 * n), f32),
        scratch_shapes=[pltpu.VMEM((n, 2 * n), f32)] if last else [],
        compiler_params=params(),
        cost_estimate=cost(0.01),
        name="factor",
    )(value)


def finish_kernel(own_ref, inverse_ref, *refs):
    parts, (out_ref, gram_ref, total) = refs[:-3], refs[-3:]
    step = total.shape[0] // SLICES
    for place in range(SLICES):
        at = pl.multiple_of((place ^ own_ref[1]) * step, step)
        row = place // 2 * step
        total[pl.ds(at, step)] = parts[place % 2][row : row + step]
    upper, rest = split(inverse_ref[...])
    stack = jnp.concatenate([upper, rest], 0)
    width = upper.shape[0]
    gram = jnp.zeros((2 * width, width), f32)
    for t in range(total.shape[1] // TILE):
        tile = slice(t * TILE, (t + 1) * TILE)
        t_upper, t_rest = split(total[:, tile])
        both = jnp.dot(stack, t_upper, preferred_element_type=f32)
        value = both[:width] + both[width:] + jnp.dot(upper, t_rest, preferred_element_type=f32)
        out_ref[:, tile] = value
        v_upper, v_rest = split(value)
        gram += lax.dot_general(
            jnp.concatenate([v_upper, v_rest], 0),
            v_upper,
            (((1,), (1,)), ((), ())),
            preferred_element_type=f32,
        )
    cross = gram[width:]
    gram_ref[...] = gram[:width] + (cross + cross.T)


def finish(own, inverse, parts):
    width = inverse.shape[0]
    cols = parts[0].shape[1]
    return pl.pallas_call(
        finish_kernel,
        in_specs=[SMEM] + [VMEM] * (1 + len(parts)),
        out_specs=[VMEM] * 2,
        out_shape=[
            jax.ShapeDtypeStruct((width, cols), f32),
            jax.ShapeDtypeStruct((width, width), f32),
        ],
        scratch_shapes=[pltpu.VMEM((width, cols), f32)],
        compiler_params=params(),
        cost_estimate=cost(8),
        name="finish",
    )(own, inverse, *parts)


def per_device(data, omega):
    nrow, ncol = lax.axis_size("row"), lax.axis_size("col")
    quarter = data.shape[0] // ncol
    assert ncol == 4 and quarter == 2 * PIECE and nrow >= 8
    total_rows = data.shape[0] * nrow
    own = jnp.stack([lax.axis_index("col"), lax.axis_index("row") % 8]).astype(jnp.int32)
    bits = [1 << k for k in range(nrow.bit_length() - 1)]

    data = pltpu.with_memory_space_constraint(data, pltpu.HBM)
    omega = pltpu.with_memory_space_constraint(omega, pltpu.HBM)

    part, rows3, rows2, wide = sketch(own, data, omega, (3,), (2,), True)
    pair, wide = fence((sketch_held(rows2, wide) + swap(part, "col", 1), wide))
    away = swap(pair, "col", 2)
    part, here, rows1, rows0 = sketch(own, data, wide, (1, 0))
    part_a, part_b, away = fence((swap(part[:PIECE], "col", 1), swap(part[PIECE:], "col", 1), away))
    sketched = here + jnp.concatenate([part_a, part_b], 0) + away

    third = swap(sketched, "col", 2)
    second = swap(sketched, "col", 1)
    gram = dot(sketched, sketched, 0, 0)
    far = swap(gram, "row", bits[0])
    (acc,) = project(own, rows0, sketched)
    far, acc, second = fence((far, acc, second))
    gram = gram + far
    far = swap(gram, "row", bits[1])
    (acc,) = project(own, rows1, second, acc)
    far, acc, third = fence((far, acc, third))
    gram = gram + far
    fourth = swap(third, "col", 1)
    (acc,) = project(own, rows2, third, acc)
    fourth, acc = fence((fourth, acc))
    send, keep = project(own, rows3, fourth, acc, SLICES)
    send, keep, gram = fence((send, keep, gram))

    got = swap(send, "row", 1)
    for bit in bits[2:]:
        gram = gram + swap(gram, "row", bit)
    gram = gram + swap(gram, "col", 1)
    got, state = fence((got, gram + swap(gram, "col", 2)))
    step = keep.shape[0] // 4
    quads = [keep[i * step : (i + 1) * step] + got[i * step : (i + 1) * step] for i in range(4)]
    *quads, state = fence((*quads, state))
    got = [swap(quads[i], "row", 2 * i) for i in (3, 2, 1)]
    *got, state = fence((*got, factor(0, 3, state)))
    mine = (quads[0] + got[0]) + (got[1] + got[2])
    for bit in bits[3:]:
        mine = mine + swap(mine, "row", bit)
    mine, state = fence((mine, state))
    got = [swap(mine, "row", 2 * i) for i in (1, 2, 3)]
    *got, state = fence((*got, factor(1, 3, state)))
    keep = jnp.concatenate([mine, *got], 0)
    keep, state = fence((keep, state))
    got, inverse = fence((swap(keep, "row", 1), factor(2, 3, state)))
    projected, small = finish(own, inverse, [keep, got])

    across = [swap(small, "col", bit) for bit in (2, 3, 1)]
    *across, basis = fence((*across, dot(sketched, inverse, 1, 1)))
    small = (small + across[2]) + (across[0] + across[1])
    return (basis, projected, small / total_rows)


def solution(mesh):
    placed = (P("row", "col"), P("col", None))
    return jax.shard_map(
        per_device,
        mesh=mesh,
        in_specs=placed,
        out_specs=(P(("row", "col"), None), P(None, "col"), P()),
        check_vma=False,
    )
```

```python
import functools

import jax
import jax.numpy as jnp
from jax import lax
from jax.experimental import pallas as pl
from jax.experimental.pallas import tpu as pltpu
from jax.sharding import PartitionSpec as P

full = lax.Precision.HIGHEST
f32 = jnp.float32
bf16 = jnp.bfloat16

PIECE = 512
TILE = 256
RUN = 128
SLICES = 8
CUTS = ((1, 2, 4), (2, 4, 1))
SMEM = pl.BlockSpec(memory_space=pltpu.SMEM)
VMEM = pl.BlockSpec(memory_space=pltpu.VMEM)
HBM = pl.BlockSpec(memory_space=pltpu.HBM)
fence = lax.optimization_barrier


def cost(mib):
    return pl.CostEstimate(flops=1, bytes_accessed=int(mib * 2**20), transcendentals=0)


def params():
    return pltpu.CompilerParams(vmem_limit_bytes=16 * 1024 * 1024)


def swap(value, axis, bit):
    return lax.ppermute(value, axis, [(i, i ^ bit) for i in range(lax.axis_size(axis))])


def stage(value, step):
    nrow, ncol = lax.axis_size("row"), lax.axis_size("col")
    pairs = [
        (r * ncol + c, (r ^ CUTS[c % 2][step]) * ncol + c) for r in range(nrow) for c in range(ncol)
    ]
    return lax.ppermute(value, ("row", "col"), pairs)


def slice_rows(own_ref, index, step):
    even, odd = [order(cut)[index] for cut in CUTS]
    place = jnp.where(own_ref[0] % 2 == 0, even, odd)
    return pl.ds(pl.multiple_of((place ^ own_ref[1]) * step, step), step)


def order(bits):
    places = [0]
    for bit in reversed(bits):
        places = places + [place ^ bit for place in places]
    return places


def dot(a, b, a_dim, b_dim, precision=full):
    return lax.dot_general(
        a, b, (((a_dim,), (b_dim,)), ((), ())), precision=precision, preferred_element_type=f32
    )


def split(value):
    upper = value.astype(bf16)
    return upper, (value - upper.astype(f32)).astype(bf16)


def multiply(held, wide, out):
    quarter, cols = held.shape
    width = out.shape[1]
    for row in range(0, quarter, PIECE):
        yield row
        for t in range(cols // TILE):
            tile = slice(t * TILE, (t + 1) * TILE)
            upper, rest = split(held[row : row + PIECE, tile])
            one = jnp.dot(upper, wide[tile, :], preferred_element_type=f32)
            two = jnp.dot(rest, wide[tile, :width], preferred_element_type=f32)
            both, more = (one, two) if t == 0 else (both + one, more + two)
        out[row : row + PIECE] = both[:, :width] + both[:, width:] + more


def sketch_kernel(places, ahead, first, own_ref, data_ref, omega_ref, *refs):
    count, total = len(places), len(places) + len(ahead)
    if first:
        refs, (omega_held, omega_sem) = refs[:-2], refs[-2:]
        omega_copy = pltpu.make_async_copy(omega_ref, omega_held, omega_sem)
        omega_copy.start()
    outs, held, sems = refs[:count], refs[count : count + total], refs[-1]
    quarter = held[0].shape[0]
    copies = {}
    for k, place in enumerate(places + ahead):
        for row in range(0, quarter, RUN):
            at = pl.multiple_of((own_ref[0] ^ place) * quarter + row, RUN)
            copy = pltpu.make_async_copy(
                data_ref.at[pl.ds(at, RUN)], held[k].at[pl.ds(row, RUN)], sems.at[k, row // RUN]
            )
            copy.start()
            copies[k, row] = copy
    if first:
        width = omega_ref.shape[1]
        wide = refs[count + total]
        omega_copy.wait()
        upper, rest = split(omega_held[...])
        wide[:, :width] = upper
        wide[:, width:] = rest
    else:
        wide = omega_ref
    for k in range(count):
        for row in multiply(held[k], wide, outs[k]):
            for run in range(row, row + PIECE, RUN):
                copies[k, run].wait()
    for k in range(count, total):
        for row in range(0, quarter, RUN):
            copies[k, row].wait()


def sketch(own, data, omega, places, ahead=(), first=False):
    cols = data.shape[1]
    width = omega.shape[1] if first else omega.shape[1] // 2
    quarter = data.shape[0] // lax.axis_size("col")
    total = len(places) + len(ahead)
    out = [jax.ShapeDtypeStruct((quarter, width), f32)] * len(places)
    out += [pltpu.VMEM((quarter, cols), f32)] * total
    scratch = [pltpu.SemaphoreType.DMA((total, quarter // RUN))]
    if first:
        out.append(jax.ShapeDtypeStruct((cols, 2 * width), bf16))
        scratch += [pltpu.VMEM(omega.shape, f32), pltpu.SemaphoreType.DMA]
    return pl.pallas_call(
        functools.partial(sketch_kernel, places, ahead, first),
        in_specs=[SMEM, HBM, HBM if first else VMEM],
        out_specs=[VMEM] * len(out),
        out_shape=out,
        scratch_shapes=scratch,
        compiler_params=params(),
        cost_estimate=cost(0.01),
        name="partial_sketch",
    )(own, data, omega)


def held_kernel(rows_ref, wide_ref, out_ref):
    for _ in multiply(rows_ref, wide_ref, out_ref):
        pass


def sketch_held(rows, wide):
    return pl.pallas_call(
        held_kernel,
        in_specs=[VMEM] * 2,
        out_specs=VMEM,
        out_shape=jax.ShapeDtypeStruct((rows.shape[0], wide.shape[1] // 2), f32),
        compiler_params=params(),
        cost_estimate=cost(0.01),
        name="partial_sketch_held",
    )(rows, wide)


def project_kernel(start, before, slices, own_ref, rows_ref, part_ref, *refs):
    old, refs = (refs[0], refs[1:]) if before else (None, refs)
    outs, total = (refs[:-1], refs[-1]) if slices else (refs, refs[0])
    cols = rows_ref.shape[1]
    for row in range(0, part_ref.shape[0], PIECE):
        upper, rest = split(part_ref[row : row + PIECE].T)
        stack = jnp.concatenate([upper, rest], 0)
        width = upper.shape[0]
        for t in range(cols // TILE):
            tile = slice(t * TILE, (t + 1) * TILE)
            d_upper, d_rest = split(rows_ref[start + row : start + row + PIECE, tile])
            both = jnp.dot(stack, d_upper, preferred_element_type=f32)
            value = both[:width] + both[width:] + jnp.dot(upper, d_rest, preferred_element_type=f32)
            if row > 0:
                value += total[:, tile]
            elif before:
                value += old[:, tile]
            total[:, tile] = value
    if slices:
        step = total.shape[0] // slices
        for index in range(slices):
            row = index % (slices // 2) * step
            keep = index < slices // 2
            outs[1 if keep else 0][row : row + step] = total[slice_rows(own_ref, index, step)]


def project(own, rows, part, before=None, slices=0, start=0):
    cols = rows.shape[1]
    width = part.shape[1]
    args = [own, rows, part] + ([] if before is None else [before])
    if slices:
        out = [jax.ShapeDtypeStruct((width // 2, cols), f32)] * 2
    else:
        out = [jax.ShapeDtypeStruct((width, cols), f32)]
    return pl.pallas_call(
        functools.partial(project_kernel, start, before is not None, slices),
        in_specs=[SMEM] + [VMEM] * (len(args) - 1),
        out_specs=[VMEM] * len(out),
        out_shape=out,
        scratch_shapes=[pltpu.VMEM((width, cols), f32)] if slices else [],
        compiler_params=params(),
        cost_estimate=cost(6 * part.shape[0] / rows.shape[0]),
        name="project",
    )(*args)


def factor_kernel(index, count, in_ref, out_ref, *scratch):
    n = in_ref.shape[0]
    last = index == count - 1
    work = scratch[0] if last else out_ref
    if index == 0:
        row = lax.broadcasted_iota(jnp.int32, (n, n), 0)
        col = lax.broadcasted_iota(jnp.int32, (n, n), 1)
        work[:, :n] = in_ref[...]
        work[:, n:] = jnp.where(row == col, 1.0, 0.0).astype(f32)
    else:
        work[...] = in_ref[...]
    sub = lax.broadcasted_iota(jnp.int32, (8, n), 0)
    panels = n // 8
    for b in range(panels * index // count, panels * (index + 1) // count):
        top = slice(8 * b, 8 * b + 8)
        panel = work[top, :]
        spread = [jnp.broadcast_to(panel[:, 8 * b + j : 8 * b + j + 1], (8, n)) for j in range(8)]
        e = [
            [jnp.broadcast_to(spread[j][i : i + 1, :], (8, n)) for j in range(i + 1)]
            for i in range(8)
        ]
        left = [jnp.broadcast_to(panel[i : i + 1, :n], (8, n)) for i in range(8)]
        right = [jnp.broadcast_to(panel[i : i + 1, n:], (8, n)) for i in range(8)]
        for j in range(8):
            scale = lax.rsqrt(e[j][j])
            left[j] = left[j] * scale
            right[j] = right[j] * scale
            low = {i: e[i][j] * scale for i in range(j + 1, 8)}
            for i in range(j + 1, 8):
                for k in range(j + 1, i + 1):
                    e[i][k] = e[i][k] - low[i] * low[k]
                left[i] = left[i] - low[i] * left[j]
                right[i] = right[i] - low[i] * right[j]
        l_panel, r_panel = left[0], right[0]
        for i in range(1, 8):
            l_panel = jnp.where(sub == i, left[i], l_panel)
            r_panel = jnp.where(sub == i, right[i], r_panel)
        work[top, n:] = r_panel
        if b < panels - 1:
            rows = slice(8 * b + 8, 8 * b + 16)
            l_next, r_next = work[rows, :n], work[rows, n:]
            column = l_panel.T[rows, :]
            for j in range(8):
                factors = jnp.broadcast_to(column[:, j : j + 1], (8, n))
                l_next = l_next - factors * left[j]
                r_next = r_next - factors * right[j]
            work[rows, :n] = l_next
            work[rows, n:] = r_next
        if b < panels - 2:
            done = jnp.concatenate([l_panel, r_panel], 1)
            change = dot(l_panel, done, 0, 0)
            below = slice(8 * b + 16, n)
            work[below, :] = work[below, :] - change[8 * b + 16 :, :]
    if last:
        out_ref[...] = work[:, n:]


def factor(index, count, value):
    n = value.shape[0]
    last = index == count - 1
    return pl.pallas_call(
        functools.partial(factor_kernel, index, count),
        in_specs=[VMEM],
        out_specs=VMEM,
        out_shape=jax.ShapeDtypeStruct((n, n if last else 2 * n), f32),
        scratch_shapes=[pltpu.VMEM((n, 2 * n), f32)] if last else [],
        compiler_params=params(),
        cost_estimate=cost(0.01),
        name="factor",
    )(value)


def finish_kernel(own_ref, inverse_ref, *refs):
    parts, (out_ref, gram_ref, total) = refs[:-3], refs[-3:]
    step = total.shape[0] // SLICES
    for index in range(SLICES):
        row = index % (SLICES // 2) * step
        half = index // (SLICES // 2)
        total[slice_rows(own_ref, index, step)] = parts[half][row : row + step]
    upper, rest = split(inverse_ref[...])
    stack = jnp.concatenate([upper, rest], 0)
    width = upper.shape[0]
    gram = jnp.zeros((2 * width, width), f32)
    for t in range(total.shape[1] // TILE):
        tile = slice(t * TILE, (t + 1) * TILE)
        t_upper, t_rest = split(total[:, tile])
        both = jnp.dot(stack, t_upper, preferred_element_type=f32)
        value = both[:width] + both[width:] + jnp.dot(upper, t_rest, preferred_element_type=f32)
        out_ref[:, tile] = value
        v_upper, v_rest = split(value)
        gram += lax.dot_general(
            jnp.concatenate([v_upper, v_rest], 0),
            v_upper,
            (((1,), (1,)), ((), ())),
            preferred_element_type=f32,
        )
    cross = gram[width:]
    gram_ref[...] = gram[:width] + (cross + cross.T)


def finish(own, inverse, parts):
    width = inverse.shape[0]
    cols = parts[0].shape[1]
    return pl.pallas_call(
        finish_kernel,
        in_specs=[SMEM] + [VMEM] * (1 + len(parts)),
        out_specs=[VMEM] * 2,
        out_shape=[
            jax.ShapeDtypeStruct((width, cols), f32),
            jax.ShapeDtypeStruct((width, width), f32),
        ],
        scratch_shapes=[pltpu.VMEM((width, cols), f32)],
        compiler_params=params(),
        cost_estimate=cost(8),
        name="finish",
    )(own, inverse, *parts)


def per_device(data, omega):
    nrow, ncol = lax.axis_size("row"), lax.axis_size("col")
    quarter = data.shape[0] // ncol
    assert ncol == 4 and quarter == 2 * PIECE and nrow >= 8
    total_rows = data.shape[0] * nrow
    own = jnp.stack([lax.axis_index("col"), lax.axis_index("row") % 8]).astype(jnp.int32)
    bits = [1 << k for k in range(nrow.bit_length() - 1)]

    data = pltpu.with_memory_space_constraint(data, pltpu.HBM)
    omega = pltpu.with_memory_space_constraint(omega, pltpu.HBM)

    part, rows3, rows2, wide = sketch(own, data, omega, (3,), (2,), True)
    pair, wide = fence((sketch_held(rows2, wide) + swap(part, "col", 1), wide))
    away = swap(pair, "col", 2)
    part, here, rows1, rows0 = sketch(own, data, wide, (1, 0))
    part_a, part_b, away = fence((swap(part[:PIECE], "col", 1), swap(part[PIECE:], "col", 1), away))
    sketched = here + jnp.concatenate([part_a, part_b], 0) + away

    third = swap(sketched, "col", 2)
    second = swap(sketched, "col", 1)
    gram = dot(sketched, sketched, 0, 0)
    far = swap(gram, "row", bits[2])
    (acc,) = project(own, rows0, sketched)
    far, acc, second = fence((far, acc, second))
    gram = gram + far
    far = swap(gram, "row", bits[1])
    (acc,) = project(own, rows1, second, acc)
    far, acc = fence((far, acc))
    gram = gram + far
    for bit in bits[3:]:
        gram = gram + swap(gram, "row", bit)
    far = swap(gram, "row", bits[0])
    third, acc, far = fence((third, acc, far))
    gram = gram + far
    fourth = swap(third, "col", 1)
    (acc,) = project(own, rows2, third, acc)
    fourth, acc = fence((fourth, acc))
    far = swap(gram, "col", 1)
    send, keep = project(own, rows3, fourth, acc, SLICES)
    far, send, keep = fence((far, send, keep))
    gram = gram + far

    got, state = fence((stage(send, 0), gram + swap(gram, "col", 2)))
    keep = keep + got
    for step in (1, 2):
        half = keep.shape[0] // 2
        keep, send, state = fence((keep[:half], keep[half:], state))
        got, state = fence((stage(send, step), factor(step - 1, 3, state)))
        keep = keep + got
    for bit in bits[3:]:
        keep = keep + swap(keep, "row", bit)
    keep, state = fence((keep, state))
    got, inverse = fence((stage(keep, 2), factor(2, 3, state)))
    keep, inverse = fence((jnp.concatenate([keep, got], 0), inverse))
    got, basis = fence((stage(keep, 1), dot(sketched, inverse, 1, 1)))
    keep, inverse = fence((jnp.concatenate([keep, got], 0), inverse))
    got = stage(keep, 0)
    projected, small = finish(own, inverse, [keep, got])

    across = [swap(small, "col", bit) for bit in (2, 3, 1)]
    small = (small + across[2]) + (across[0] + across[1])
    return (basis, projected, small / total_rows)


def solution(mesh):
    placed = (P("row", "col"), P("col", None))
    return jax.shard_map(
        per_device,
        mesh=mesh,
        in_specs=placed,
        out_specs=(P(("row", "col"), None), P(None, "col"), P()),
        check_vma=False,
    )
```

```python
import functools

import jax
import jax.numpy as jnp
from jax import lax
from jax.experimental import pallas as pl
from jax.experimental.pallas import tpu as pltpu
from jax.sharding import PartitionSpec as P

full = lax.Precision.HIGHEST
f32 = jnp.float32
bf16 = jnp.bfloat16

PIECE = 512
TILE = 256
RUN = 128
SLICES = 8
SMEM = pl.BlockSpec(memory_space=pltpu.SMEM)
VMEM = pl.BlockSpec(memory_space=pltpu.VMEM)
HBM = pl.BlockSpec(memory_space=pltpu.HBM)
fence = lax.optimization_barrier


def cost(mib):
    return pl.CostEstimate(flops=1, bytes_accessed=int(mib * 2**20), transcendentals=0)


def params():
    return pltpu.CompilerParams(vmem_limit_bytes=16 * 1024 * 1024)


def swap(value, axis, bit):
    return lax.ppermute(value, axis, [(i, i ^ bit) for i in range(lax.axis_size(axis))])


def dot(a, b, a_dim, b_dim, precision=full):
    return lax.dot_general(
        a, b, (((a_dim,), (b_dim,)), ((), ())), precision=precision, preferred_element_type=f32
    )


def split(value):
    upper = value.astype(bf16)
    return upper, (value - upper.astype(f32)).astype(bf16)


def multiply(held, wide, out):
    quarter, cols = held.shape
    width = out.shape[1]
    for row in range(0, quarter, PIECE):
        yield row
        for t in range(cols // TILE):
            tile = slice(t * TILE, (t + 1) * TILE)
            upper, rest = split(held[row : row + PIECE, tile])
            one = jnp.dot(upper, wide[tile, :], preferred_element_type=f32)
            two = jnp.dot(rest, wide[tile, :width], preferred_element_type=f32)
            both, more = (one, two) if t == 0 else (both + one, more + two)
        out[row : row + PIECE] = both[:, :width] + both[:, width:] + more


def sketch_kernel(places, ahead, first, own_ref, data_ref, omega_ref, *refs):
    count, total = len(places), len(places) + len(ahead)
    if first:
        refs, (omega_held, omega_sem) = refs[:-2], refs[-2:]
        omega_copy = pltpu.make_async_copy(omega_ref, omega_held, omega_sem)
        omega_copy.start()
    outs, held, sems = refs[:count], refs[count : count + total], refs[-1]
    quarter = held[0].shape[0]
    copies = {}
    for k, place in enumerate(places + ahead):
        for row in range(0, quarter, RUN):
            at = pl.multiple_of((own_ref[0] ^ place) * quarter + row, RUN)
            copy = pltpu.make_async_copy(
                data_ref.at[pl.ds(at, RUN)], held[k].at[pl.ds(row, RUN)], sems.at[k, row // RUN]
            )
            copy.start()
            copies[k, row] = copy
    if first:
        width = omega_ref.shape[1]
        wide = refs[count + total]
        omega_copy.wait()
        upper, rest = split(omega_held[...])
        wide[:, :width] = upper
        wide[:, width:] = rest
    else:
        wide = omega_ref
    for k in range(count):
        for row in multiply(held[k], wide, outs[k]):
            for run in range(row, row + PIECE, RUN):
                copies[k, run].wait()
    for k in range(count, total):
        for row in range(0, quarter, RUN):
            copies[k, row].wait()


def sketch(own, data, omega, places, ahead=(), first=False):
    cols = data.shape[1]
    width = omega.shape[1] if first else omega.shape[1] // 2
    quarter = data.shape[0] // lax.axis_size("col")
    total = len(places) + len(ahead)
    out = [jax.ShapeDtypeStruct((quarter, width), f32)] * len(places)
    out += [pltpu.VMEM((quarter, cols), f32)] * total
    scratch = [pltpu.SemaphoreType.DMA((total, quarter // RUN))]
    if first:
        out.append(jax.ShapeDtypeStruct((cols, 2 * width), bf16))
        scratch += [pltpu.VMEM(omega.shape, f32), pltpu.SemaphoreType.DMA]
    return pl.pallas_call(
        functools.partial(sketch_kernel, places, ahead, first),
        in_specs=[SMEM, HBM, HBM if first else VMEM],
        out_specs=[VMEM] * len(out),
        out_shape=out,
        scratch_shapes=scratch,
        compiler_params=params(),
        cost_estimate=cost(0.01),
        name="partial_sketch",
    )(own, data, omega)


def held_kernel(rows_ref, wide_ref, out_ref):
    for _ in multiply(rows_ref, wide_ref, out_ref):
        pass


def sketch_held(rows, wide):
    return pl.pallas_call(
        held_kernel,
        in_specs=[VMEM] * 2,
        out_specs=VMEM,
        out_shape=jax.ShapeDtypeStruct((rows.shape[0], wide.shape[1] // 2), f32),
        compiler_params=params(),
        cost_estimate=cost(0.01),
        name="partial_sketch_held",
    )(rows, wide)


def project_kernel(start, before, slices, own_ref, rows_ref, part_ref, *refs):
    old, refs = (refs[0], refs[1:]) if before else (None, refs)
    outs, total = (refs[:-1], refs[-1]) if slices else (refs, refs[0])
    cols = rows_ref.shape[1]
    for row in range(0, part_ref.shape[0], PIECE):
        upper, rest = split(part_ref[row : row + PIECE].T)
        stack = jnp.concatenate([upper, rest], 0)
        width = upper.shape[0]
        for t in range(cols // TILE):
            tile = slice(t * TILE, (t + 1) * TILE)
            d_upper, d_rest = split(rows_ref[start + row : start + row + PIECE, tile])
            both = jnp.dot(stack, d_upper, preferred_element_type=f32)
            value = both[:width] + both[width:] + jnp.dot(upper, d_rest, preferred_element_type=f32)
            if row > 0:
                value += total[:, tile]
            elif before:
                value += old[:, tile]
            total[:, tile] = value
    if slices:
        step = total.shape[0] // slices
        for place in range(slices):
            at = pl.multiple_of((place ^ own_ref[1]) * step, step)
            group, row = ((0, 0), (1, 0), (1, step), (0, step))[place // 2]
            outs[2 * (place % 2) + group][row : row + step] = total[pl.ds(at, step)]


def project(own, rows, part, before=None, slices=0, start=0):
    cols = rows.shape[1]
    width = part.shape[1]
    args = [own, rows, part] + ([] if before is None else [before])
    if slices:
        out = [jax.ShapeDtypeStruct((width // 4, cols), f32)] * 4
    else:
        out = [jax.ShapeDtypeStruct((width, cols), f32)]
    return pl.pallas_call(
        functools.partial(project_kernel, start, before is not None, slices),
        in_specs=[SMEM] + [VMEM] * (len(args) - 1),
        out_specs=[VMEM] * len(out),
        out_shape=out,
        scratch_shapes=[pltpu.VMEM((width, cols), f32)] if slices else [],
        compiler_params=params(),
        cost_estimate=cost(6 * part.shape[0] / rows.shape[0]),
        name="project",
    )(*args)


def factor_kernel(index, count, in_ref, out_ref, *scratch):
    n = in_ref.shape[0]
    last = index == count - 1
    work = scratch[0] if last else out_ref
    if index == 0:
        row = lax.broadcasted_iota(jnp.int32, (n, n), 0)
        col = lax.broadcasted_iota(jnp.int32, (n, n), 1)
        work[:, :n] = in_ref[...]
        work[:, n:] = jnp.where(row == col, 1.0, 0.0).astype(f32)
    else:
        work[...] = in_ref[...]
    sub = lax.broadcasted_iota(jnp.int32, (8, n), 0)
    panels = n // 8
    for b in range(panels * index // count, panels * (index + 1) // count):
        top = slice(8 * b, 8 * b + 8)
        panel = work[top, :]
        spread = [jnp.broadcast_to(panel[:, 8 * b + j : 8 * b + j + 1], (8, n)) for j in range(8)]
        e = [
            [jnp.broadcast_to(spread[j][i : i + 1, :], (8, n)) for j in range(i + 1)]
            for i in range(8)
        ]
        left = [jnp.broadcast_to(panel[i : i + 1, :n], (8, n)) for i in range(8)]
        right = [jnp.broadcast_to(panel[i : i + 1, n:], (8, n)) for i in range(8)]
        for j in range(8):
            scale = lax.rsqrt(e[j][j])
            left[j] = left[j] * scale
            right[j] = right[j] * scale
            low = {i: e[i][j] * scale for i in range(j + 1, 8)}
            for i in range(j + 1, 8):
                for k in range(j + 1, i + 1):
                    e[i][k] = e[i][k] - low[i] * low[k]
                left[i] = left[i] - low[i] * left[j]
                right[i] = right[i] - low[i] * right[j]
        l_panel, r_panel = left[0], right[0]
        for i in range(1, 8):
            l_panel = jnp.where(sub == i, left[i], l_panel)
            r_panel = jnp.where(sub == i, right[i], r_panel)
        work[top, n:] = r_panel
        if b < panels - 1:
            rows = slice(8 * b + 8, 8 * b + 16)
            l_next, r_next = work[rows, :n], work[rows, n:]
            column = l_panel.T[rows, :]
            for j in range(8):
                factors = jnp.broadcast_to(column[:, j : j + 1], (8, n))
                l_next = l_next - factors * left[j]
                r_next = r_next - factors * right[j]
            work[rows, :n] = l_next
            work[rows, n:] = r_next
        if b < panels - 2:
            done = jnp.concatenate([l_panel, r_panel], 1)
            change = dot(l_panel, done, 0, 0)
            below = slice(8 * b + 16, n)
            work[below, :] = work[below, :] - change[8 * b + 16 :, :]
    if last:
        out_ref[...] = work[:, n:]


def factor(index, count, value):
    n = value.shape[0]
    last = index == count - 1
    return pl.pallas_call(
        functools.partial(factor_kernel, index, count),
        in_specs=[VMEM],
        out_specs=VMEM,
        out_shape=jax.ShapeDtypeStruct((n, n if last else 2 * n), f32),
        scratch_shapes=[pltpu.VMEM((n, 2 * n), f32)] if last else [],
        compiler_params=params(),
        cost_estimate=cost(0.01),
        name="factor",
    )(value)


def finish_kernel(own_ref, inverse_ref, *refs):
    parts, (out_ref, gram_ref, total) = refs[:-3], refs[-3:]
    step = total.shape[0] // SLICES
    for place in range(SLICES):
        at = pl.multiple_of((place ^ own_ref[1]) * step, step)
        row = place // 2 * step
        total[pl.ds(at, step)] = parts[place % 2][row : row + step]
    upper, rest = split(inverse_ref[...])
    stack = jnp.concatenate([upper, rest], 0)
    width = upper.shape[0]
    gram = jnp.zeros((2 * width, width), f32)
    for t in range(total.shape[1] // TILE):
        tile = slice(t * TILE, (t + 1) * TILE)
        t_upper, t_rest = split(total[:, tile])
        both = jnp.dot(stack, t_upper, preferred_element_type=f32)
        value = both[:width] + both[width:] + jnp.dot(upper, t_rest, preferred_element_type=f32)
        out_ref[:, tile] = value
        v_upper, v_rest = split(value)
        gram += lax.dot_general(
            jnp.concatenate([v_upper, v_rest], 0),
            v_upper,
            (((1,), (1,)), ((), ())),
            preferred_element_type=f32,
        )
    cross = gram[width:]
    gram_ref[...] = gram[:width] + (cross + cross.T)


def finish(own, inverse, parts):
    width = inverse.shape[0]
    cols = parts[0].shape[1]
    return pl.pallas_call(
        finish_kernel,
        in_specs=[SMEM] + [VMEM] * (1 + len(parts)),
        out_specs=[VMEM] * 2,
        out_shape=[
            jax.ShapeDtypeStruct((width, cols), f32),
            jax.ShapeDtypeStruct((width, width), f32),
        ],
        scratch_shapes=[pltpu.VMEM((width, cols), f32)],
        compiler_params=params(),
        cost_estimate=cost(8),
        name="finish",
    )(own, inverse, *parts)


def per_device(data, omega):
    nrow, ncol = lax.axis_size("row"), lax.axis_size("col")
    quarter = data.shape[0] // ncol
    assert ncol == 4 and quarter == 2 * PIECE and nrow >= 8
    total_rows = data.shape[0] * nrow
    own = jnp.stack([lax.axis_index("col"), lax.axis_index("row") % 8]).astype(jnp.int32)
    bits = [1 << k for k in range(nrow.bit_length() - 1)]

    data = pltpu.with_memory_space_constraint(data, pltpu.HBM)
    omega = pltpu.with_memory_space_constraint(omega, pltpu.HBM)

    part, rows3, rows2, wide = sketch(own, data, omega, (3,), (2,), True)
    pair, wide = fence((sketch_held(rows2, wide) + swap(part, "col", 1), wide))
    away = swap(pair, "col", 2)
    part, here, rows1, rows0 = sketch(own, data, wide, (1, 0))
    part_a, part_b, away = fence((swap(part[:PIECE], "col", 1), swap(part[PIECE:], "col", 1), away))
    sketched = here + jnp.concatenate([part_a, part_b], 0) + away

    third = swap(sketched, "col", 2)
    second = swap(sketched, "col", 1)
    gram = dot(sketched, sketched, 0, 0)
    far = swap(gram, "row", bits[0])
    (acc,) = project(own, rows0, sketched)
    far, acc, second = fence((far, acc, second))
    gram = gram + far
    far = swap(gram, "row", bits[1])
    (acc,) = project(own, rows1, second, acc)
    far, acc = fence((far, acc))
    gram = gram + far
    far = swap(gram, "row", bits[2])
    third, acc, far = fence((third, acc, far))
    gram = gram + far
    for bit in bits[3:]:
        gram = gram + swap(gram, "row", bit)
    fourth = swap(third, "col", 1)
    (acc,) = project(own, rows2, third, acc)
    fourth, acc = fence((fourth, acc))
    far = swap(gram, "col", 1)
    outer_keep, inner_keep, outer_send, inner_send = project(own, rows3, fourth, acc, SLICES)
    far, outer_keep, inner_keep, outer_send, inner_send = fence(
        (far, outer_keep, inner_keep, outer_send, inner_send)
    )
    gram = gram + far

    step = outer_keep.shape[0] // 2
    outer_got, state = fence((swap(outer_send, "row", 1), gram + swap(gram, "col", 2)))
    zero, six = outer_keep[:step] + outer_got[:step], outer_keep[step:] + outer_got[step:]
    zero, six, state = fence((zero, six, state))
    six = swap(six, "row", 6)
    inner_got = swap(inner_send, "row", 1)
    two, four = inner_keep[:step] + inner_got[:step], inner_keep[step:] + inner_got[step:]
    four, two = swap(four, "row", 4), swap(two, "row", 2)
    six, four, two, state = fence((six, four, two, factor(0, 3, state)))
    zero = (zero + two) + (four + six)
    for bit in bits[3:]:
        zero = zero + swap(zero, "row", bit)
    zero, state = fence((zero, state))
    got = [swap(zero, "row", q) for q in (2, 4, 6)]
    *got, state = fence((*got, factor(1, 3, state)))
    keep, state = fence((jnp.concatenate([zero, *got], 0), state))
    got, inverse = fence((swap(keep, "row", 1), factor(2, 3, state)))
    projected, small = finish(own, inverse, [keep, got])

    across = [swap(small, "col", bit) for bit in (2, 3, 1)]
    *across, basis = fence((*across, dot(sketched, inverse, 1, 1)))
    small = (small + across[2]) + (across[0] + across[1])
    return (basis, projected, small / total_rows)


def solution(mesh):
    placed = (P("row", "col"), P("col", None))
    return jax.shard_map(
        per_device,
        mesh=mesh,
        in_specs=placed,
        out_specs=(P(("row", "col"), None), P(None, "col"), P()),
        check_vma=False,
    )
```

```python
import functools

import jax
import jax.numpy as jnp
from jax import lax
from jax.experimental import pallas as pl
from jax.experimental.pallas import tpu as pltpu
from jax.sharding import PartitionSpec as P

full = lax.Precision.HIGHEST
f32 = jnp.float32
bf16 = jnp.bfloat16

PIECE = 512
TILE = 256
RUN = 512
SLICES = 8
SMEM = pl.BlockSpec(memory_space=pltpu.SMEM)
VMEM = pl.BlockSpec(memory_space=pltpu.VMEM)
HBM = pl.BlockSpec(memory_space=pltpu.HBM)
fence = lax.optimization_barrier


def cost(mib):
    return pl.CostEstimate(flops=1, bytes_accessed=int(mib * 2**20), transcendentals=0)


def params():
    return pltpu.CompilerParams(vmem_limit_bytes=16 * 1024 * 1024)


def swap(value, axis, bit):
    return lax.ppermute(value, axis, [(i, i ^ bit) for i in range(lax.axis_size(axis))])


def dot(a, b, a_dim, b_dim, precision=full):
    return lax.dot_general(
        a, b, (((a_dim,), (b_dim,)), ((), ())), precision=precision, preferred_element_type=f32
    )


def split(value):
    upper = value.astype(bf16)
    return upper, (value - upper.astype(f32)).astype(bf16)


def multiply(held, wide, out):
    quarter, cols = held.shape
    width = out.shape[1]
    for row in range(0, quarter, PIECE):
        yield row
        for t in range(cols // TILE):
            tile = slice(t * TILE, (t + 1) * TILE)
            upper, rest = split(held[row : row + PIECE, tile])
            one = jnp.dot(upper, wide[tile, :], preferred_element_type=f32)
            two = jnp.dot(rest, wide[tile, :width], preferred_element_type=f32)
            both, more = (one, two) if t == 0 else (both + one, more + two)
        out[row : row + PIECE] = both[:, :width] + both[:, width:] + more


def sketch_kernel(places, ahead, first, own_ref, data_ref, omega_ref, *refs):
    count, total = len(places), len(places) + len(ahead)
    if first:
        refs, (omega_held, omega_sem) = refs[:-2], refs[-2:]
        omega_copy = pltpu.make_async_copy(omega_ref, omega_held, omega_sem)
        omega_copy.start()
    outs, held, sems = refs[:count], refs[count : count + total], refs[-1]
    quarter = held[0].shape[0]
    copies = {}
    for k, place in enumerate(places + ahead):
        for row in range(0, quarter, RUN):
            at = pl.multiple_of((own_ref[0] ^ place) * quarter + row, RUN)
            copy = pltpu.make_async_copy(
                data_ref.at[pl.ds(at, RUN)], held[k].at[pl.ds(row, RUN)], sems.at[k, row // RUN]
            )
            copy.start()
            copies[k, row] = copy
    if first:
        width = omega_ref.shape[1]
        wide = refs[count + total]
        omega_copy.wait()
        upper, rest = split(omega_held[...])
        wide[:, :width] = upper
        wide[:, width:] = rest
    else:
        wide = omega_ref
    for k in range(count):
        for row in multiply(held[k], wide, outs[k]):
            for run in range(row, row + PIECE, RUN):
                copies[k, run].wait()
    for k in range(count, total):
        for row in range(0, quarter, RUN):
            copies[k, row].wait()


def sketch(own, data, omega, places, ahead=(), first=False):
    cols = data.shape[1]
    width = omega.shape[1] if first else omega.shape[1] // 2
    quarter = data.shape[0] // lax.axis_size("col")
    total = len(places) + len(ahead)
    out = [jax.ShapeDtypeStruct((quarter, width), f32)] * len(places)
    out += [pltpu.VMEM((quarter, cols), f32)] * total
    scratch = [pltpu.SemaphoreType.DMA((total, quarter // RUN))]
    if first:
        out.append(jax.ShapeDtypeStruct((cols, 2 * width), bf16))
        scratch += [pltpu.VMEM(omega.shape, f32), pltpu.SemaphoreType.DMA]
    return pl.pallas_call(
        functools.partial(sketch_kernel, places, ahead, first),
        in_specs=[SMEM, HBM, HBM if first else VMEM],
        out_specs=[VMEM] * len(out),
        out_shape=out,
        scratch_shapes=scratch,
        compiler_params=params(),
        cost_estimate=cost(0.01),
        name="partial_sketch",
    )(own, data, omega)


def held_kernel(rows_ref, wide_ref, out_ref):
    for _ in multiply(rows_ref, wide_ref, out_ref):
        pass


def sketch_held(rows, wide):
    return pl.pallas_call(
        held_kernel,
        in_specs=[VMEM] * 2,
        out_specs=VMEM,
        out_shape=jax.ShapeDtypeStruct((rows.shape[0], wide.shape[1] // 2), f32),
        compiler_params=params(),
        cost_estimate=cost(0.01),
        name="partial_sketch_held",
    )(rows, wide)


def project_kernel(start, before, slices, own_ref, rows_ref, part_ref, *refs):
    old, refs = (refs[0], refs[1:]) if before else (None, refs)
    outs, total = (refs[:-1], refs[-1]) if slices else (refs, refs[0])
    cols = rows_ref.shape[1]
    for row in range(0, part_ref.shape[0], PIECE):
        upper, rest = split(part_ref[row : row + PIECE].T)
        stack = jnp.concatenate([upper, rest], 0)
        width = upper.shape[0]
        for t in range(cols // TILE):
            tile = slice(t * TILE, (t + 1) * TILE)
            d_upper, d_rest = split(rows_ref[start + row : start + row + PIECE, tile])
            both = jnp.dot(stack, d_upper, preferred_element_type=f32)
            value = both[:width] + both[width:] + jnp.dot(upper, d_rest, preferred_element_type=f32)
            if row > 0:
                value += total[:, tile]
            elif before:
                value += old[:, tile]
            total[:, tile] = value
    if slices:
        step = total.shape[0] // slices
        for place in range(slices):
            at = pl.multiple_of((place ^ own_ref[1]) * step, step)
            group, row = ((0, 0), (1, 0), (1, step), (0, step))[place // 2]
            outs[2 * (place % 2) + group][row : row + step] = total[pl.ds(at, step)]


def project(own, rows, part, before=None, slices=0, start=0):
    cols = rows.shape[1]
    width = part.shape[1]
    args = [own, rows, part] + ([] if before is None else [before])
    if slices:
        out = [jax.ShapeDtypeStruct((width // 4, cols), f32)] * 4
    else:
        out = [jax.ShapeDtypeStruct((width, cols), f32)]
    return pl.pallas_call(
        functools.partial(project_kernel, start, before is not None, slices),
        in_specs=[SMEM] + [VMEM] * (len(args) - 1),
        out_specs=[VMEM] * len(out),
        out_shape=out,
        scratch_shapes=[pltpu.VMEM((width, cols), f32)] if slices else [],
        compiler_params=params(),
        cost_estimate=cost(6 * part.shape[0] / rows.shape[0]),
        name="project",
    )(*args)


def factor_kernel(first, end, in_ref, out_ref, *scratch):
    n = in_ref.shape[0]
    panels = n // 8
    last = end == panels
    work = scratch[0] if last else out_ref
    if first == 0:
        row = lax.broadcasted_iota(jnp.int32, (n, n), 0)
        col = lax.broadcasted_iota(jnp.int32, (n, n), 1)
        work[:, :n] = in_ref[...]
        work[:, n:] = jnp.where(row == col, 1.0, 0.0).astype(f32)
    else:
        work[...] = in_ref[...]
    sub = lax.broadcasted_iota(jnp.int32, (8, n), 0)
    for b in range(first, end):
        top = slice(8 * b, 8 * b + 8)
        panel = work[top, :]
        spread = [jnp.broadcast_to(panel[:, 8 * b + j : 8 * b + j + 1], (8, n)) for j in range(8)]
        e = [
            [jnp.broadcast_to(spread[j][i : i + 1, :], (8, n)) for j in range(i + 1)]
            for i in range(8)
        ]
        left = [jnp.broadcast_to(panel[i : i + 1, :n], (8, n)) for i in range(8)]
        right = [jnp.broadcast_to(panel[i : i + 1, n:], (8, n)) for i in range(8)]
        for j in range(8):
            scale = lax.rsqrt(e[j][j])
            left[j] = left[j] * scale
            right[j] = right[j] * scale
            low = {i: e[i][j] * scale for i in range(j + 1, 8)}
            for i in range(j + 1, 8):
                for k in range(j + 1, i + 1):
                    e[i][k] = e[i][k] - low[i] * low[k]
                left[i] = left[i] - low[i] * left[j]
                right[i] = right[i] - low[i] * right[j]
        l_panel, r_panel = left[0], right[0]
        for i in range(1, 8):
            l_panel = jnp.where(sub == i, left[i], l_panel)
            r_panel = jnp.where(sub == i, right[i], r_panel)
        work[top, n:] = r_panel
        if b < panels - 1:
            rows = slice(8 * b + 8, 8 * b + 16)
            l_next, r_next = work[rows, :n], work[rows, n:]
            column = l_panel.T[rows, :]
            for j in range(8):
                factors = jnp.broadcast_to(column[:, j : j + 1], (8, n))
                l_next = l_next - factors * left[j]
                r_next = r_next - factors * right[j]
            work[rows, :n] = l_next
            work[rows, n:] = r_next
        if b < panels - 2:
            done = jnp.concatenate([l_panel, r_panel], 1)
            change = dot(l_panel, done, 0, 0)
            below = slice(8 * b + 16, n)
            work[below, :] = work[below, :] - change[8 * b + 16 :, :]
    if last:
        out_ref[...] = work[:, n:]


def factor(first, end, value):
    n = value.shape[0]
    last = end == n // 8
    return pl.pallas_call(
        functools.partial(factor_kernel, first, end),
        in_specs=[VMEM],
        out_specs=VMEM,
        out_shape=jax.ShapeDtypeStruct((n, n if last else 2 * n), f32),
        scratch_shapes=[pltpu.VMEM((n, 2 * n), f32)] if last else [],
        compiler_params=params(),
        cost_estimate=cost(0.01),
        name="factor",
    )(value)


def finish_kernel(own_ref, inverse_ref, *refs):
    parts, (out_ref, gram_ref, total) = refs[:-3], refs[-3:]
    step = total.shape[0] // SLICES
    for place in range(SLICES):
        at = pl.multiple_of((place ^ own_ref[1]) * step, step)
        row = place // 2 * step
        total[pl.ds(at, step)] = parts[place % 2][row : row + step]
    upper, rest = split(inverse_ref[...])
    stack = jnp.concatenate([upper, rest], 0)
    width = upper.shape[0]
    gram = jnp.zeros((2 * width, width), f32)
    for t in range(total.shape[1] // TILE):
        tile = slice(t * TILE, (t + 1) * TILE)
        t_upper, t_rest = split(total[:, tile])
        both = jnp.dot(stack, t_upper, preferred_element_type=f32)
        value = both[:width] + both[width:] + jnp.dot(upper, t_rest, preferred_element_type=f32)
        out_ref[:, tile] = value
        v_upper, v_rest = split(value)
        gram += lax.dot_general(
            jnp.concatenate([v_upper, v_rest], 0),
            v_upper,
            (((1,), (1,)), ((), ())),
            preferred_element_type=f32,
        )
    cross = gram[width:]
    gram_ref[...] = gram[:width] + (cross + cross.T)


def finish(own, inverse, parts):
    width = inverse.shape[0]
    cols = parts[0].shape[1]
    return pl.pallas_call(
        finish_kernel,
        in_specs=[SMEM] + [VMEM] * (1 + len(parts)),
        out_specs=[VMEM] * 2,
        out_shape=[
            jax.ShapeDtypeStruct((width, cols), f32),
            jax.ShapeDtypeStruct((width, width), f32),
        ],
        scratch_shapes=[pltpu.VMEM((width, cols), f32)],
        compiler_params=params(),
        cost_estimate=cost(8),
        name="finish",
    )(own, inverse, *parts)


def per_device(data, omega):
    nrow, ncol = lax.axis_size("row"), lax.axis_size("col")
    quarter = data.shape[0] // ncol
    assert ncol == 4 and quarter == 2 * PIECE and nrow >= 8
    total_rows = data.shape[0] * nrow
    own = jnp.stack([lax.axis_index("col"), lax.axis_index("row") % 8]).astype(jnp.int32)
    bits = [1 << k for k in range(nrow.bit_length() - 1)]

    data = pltpu.with_memory_space_constraint(data, pltpu.HBM)
    omega = pltpu.with_memory_space_constraint(omega, pltpu.HBM)

    part, rows3, rows2, wide = sketch(own, data, omega, (3,), (2,), True)
    pair, wide = fence((sketch_held(rows2, wide) + swap(part, "col", 1), wide))
    away = swap(pair, "col", 2)
    part, here, rows1, rows0 = sketch(own, data, wide, (1, 0))
    part_a, part_b, away = fence((swap(part[:PIECE], "col", 1), swap(part[PIECE:], "col", 1), away))
    sketched = here + jnp.concatenate([part_a, part_b], 0) + away

    third = swap(sketched, "col", 2)
    second = swap(sketched, "col", 1)
    gram = dot(sketched, sketched, 0, 0)
    far = swap(gram, "row", bits[0])
    (acc,) = project(own, rows0, sketched)
    far, acc, second = fence((far, acc, second))
    gram = gram + far
    far = swap(gram, "row", bits[1])
    (acc,) = project(own, rows1, second, acc)
    far, acc, third = fence((far, acc, third))
    gram = gram + far
    fourth = swap(third, "col", 1)
    (acc,) = project(own, rows2, third, acc)
    fourth, acc = fence((fourth, acc))
    far = swap(gram, "col", 1)
    outer_keep, inner_keep, outer_send, inner_send = project(own, rows3, fourth, acc, SLICES)
    far, outer_keep, inner_keep, outer_send, inner_send = fence(
        (far, outer_keep, inner_keep, outer_send, inner_send)
    )
    gram = gram + far

    step = outer_keep.shape[0] // 2
    outer_got = swap(outer_send, "row", 1)
    zero, six = outer_keep[:step] + outer_got[:step], outer_keep[step:] + outer_got[step:]
    zero, six = fence((zero, six))
    six = swap(six, "row", 6)
    inner_got, far = fence((swap(inner_send, "row", 1), swap(gram, "col", 2)))
    gram = gram + far
    two, four = inner_keep[:step] + inner_got[:step], inner_keep[step:] + inner_got[step:]
    four, two = swap(four, "row", 4), swap(two, "row", 2)
    for bit in bits[2:]:
        gram = gram + swap(gram, "row", bit)
    six, four, two, state = fence((six, four, two, gram))
    zero = (zero + two) + (four + six)
    for bit in bits[3:]:
        zero = zero + swap(zero, "row", bit)
    zero, state = fence((zero, state))
    got = [swap(zero, "row", q) for q in (2, 4, 6)]
    *got, state = fence((*got, factor(0, 6, state)))
    keep, state = fence((jnp.concatenate([zero, *got], 0), state))
    got, inverse = fence((swap(keep, "row", 1), factor(6, 16, state)))
    projected, small = finish(own, inverse, [keep, got])

    across = [swap(small, "col", bit) for bit in (2, 3, 1)]
    *across, basis = fence((*across, dot(sketched, inverse, 1, 1)))
    small = (small + across[2]) + (across[0] + across[1])
    return (basis, projected, small / total_rows)


def solution(mesh):
    placed = (P("row", "col"), P("col", None))
    return jax.shard_map(
        per_device,
        mesh=mesh,
        in_specs=placed,
        out_specs=(P(("row", "col"), None), P(None, "col"), P()),
        check_vma=False,
    )
```

```python
import functools

import jax
import jax.numpy as jnp
from jax import lax
from jax.experimental import pallas as pl
from jax.experimental.pallas import tpu as pltpu
from jax.sharding import PartitionSpec as P

full = lax.Precision.HIGHEST
f32 = jnp.float32
bf16 = jnp.bfloat16

PIECE = 512
TILE = 256
RUN = 512
SLICES = 8
SMEM = pl.BlockSpec(memory_space=pltpu.SMEM)
VMEM = pl.BlockSpec(memory_space=pltpu.VMEM)
HBM = pl.BlockSpec(memory_space=pltpu.HBM)
fence = lax.optimization_barrier


def cost(mib):
    return pl.CostEstimate(flops=1, bytes_accessed=int(mib * 2**20), transcendentals=0)


def params():
    return pltpu.CompilerParams(vmem_limit_bytes=16 * 1024 * 1024)


def swap(value, axis, bit):
    return lax.ppermute(value, axis, [(i, i ^ bit) for i in range(lax.axis_size(axis))])


def dot(a, b, a_dim, b_dim, precision=full):
    return lax.dot_general(
        a, b, (((a_dim,), (b_dim,)), ((), ())), precision=precision, preferred_element_type=f32
    )


def split(value):
    upper = value.astype(bf16)
    return upper, (value - upper.astype(f32)).astype(bf16)


def multiply(held, wide, out):
    quarter, cols = held.shape
    width = out.shape[1]
    for row in range(0, quarter, PIECE):
        yield row
        for t in range(cols // TILE):
            tile = slice(t * TILE, (t + 1) * TILE)
            upper, rest = split(held[row : row + PIECE, tile])
            one = jnp.dot(upper, wide[tile, :], preferred_element_type=f32)
            two = jnp.dot(rest, wide[tile, :width], preferred_element_type=f32)
            both, more = (one, two) if t == 0 else (both + one, more + two)
        out[row : row + PIECE] = both[:, :width] + both[:, width:] + more


def sketch_kernel(places, ahead, first, own_ref, data_ref, omega_ref, *refs):
    count, total = len(places), len(places) + len(ahead)
    if first:
        refs, (omega_held, omega_sem) = refs[:-2], refs[-2:]
        omega_copy = pltpu.make_async_copy(omega_ref, omega_held, omega_sem)
        omega_copy.start()
    outs, held, sems = refs[:count], refs[count : count + total], refs[-1]
    quarter = held[0].shape[0]
    copies = {}
    for k, place in enumerate(places + ahead):
        for row in range(0, quarter, RUN):
            at = pl.multiple_of((own_ref[0] ^ place) * quarter + row, RUN)
            copy = pltpu.make_async_copy(
                data_ref.at[pl.ds(at, RUN)], held[k].at[pl.ds(row, RUN)], sems.at[k, row // RUN]
            )
            copy.start()
            copies[k, row] = copy
    if first:
        width = omega_ref.shape[1]
        wide = refs[count + total]
        omega_copy.wait()
        upper, rest = split(omega_held[...])
        wide[:, :width] = upper
        wide[:, width:] = rest
    else:
        wide = omega_ref
    for k in range(count):
        for row in multiply(held[k], wide, outs[k]):
            for run in range(row, row + PIECE, RUN):
                copies[k, run].wait()
    for k in range(count, total):
        for row in range(0, quarter, RUN):
            copies[k, row].wait()


def sketch(own, data, omega, places, ahead=(), first=False):
    cols = data.shape[1]
    width = omega.shape[1] if first else omega.shape[1] // 2
    quarter = data.shape[0] // lax.axis_size("col")
    total = len(places) + len(ahead)
    out = [jax.ShapeDtypeStruct((quarter, width), f32)] * len(places)
    out += [pltpu.VMEM((quarter, cols), f32)] * total
    scratch = [pltpu.SemaphoreType.DMA((total, quarter // RUN))]
    if first:
        out.append(jax.ShapeDtypeStruct((cols, 2 * width), bf16))
        scratch += [pltpu.VMEM(omega.shape, f32), pltpu.SemaphoreType.DMA]
    return pl.pallas_call(
        functools.partial(sketch_kernel, places, ahead, first),
        in_specs=[SMEM, HBM, HBM if first else VMEM],
        out_specs=[VMEM] * len(out),
        out_shape=out,
        scratch_shapes=scratch,
        compiler_params=params(),
        cost_estimate=cost(0.01),
        name="partial_sketch",
    )(own, data, omega)


def held_kernel(rows_ref, wide_ref, out_ref):
    for _ in multiply(rows_ref, wide_ref, out_ref):
        pass


def sketch_held(rows, wide):
    return pl.pallas_call(
        held_kernel,
        in_specs=[VMEM] * 2,
        out_specs=VMEM,
        out_shape=jax.ShapeDtypeStruct((rows.shape[0], wide.shape[1] // 2), f32),
        compiler_params=params(),
        cost_estimate=cost(0.01),
        name="partial_sketch_held",
    )(rows, wide)


def project_kernel(start, before, slices, own_ref, rows_ref, part_ref, *refs):
    old, refs = (refs[0], refs[1:]) if before else (None, refs)
    outs, total = (refs[:-1], refs[-1]) if slices else (refs, refs[0])
    cols = rows_ref.shape[1]
    for row in range(0, part_ref.shape[0], PIECE):
        upper, rest = split(part_ref[row : row + PIECE].T)
        stack = jnp.concatenate([upper, rest], 0)
        width = upper.shape[0]
        for t in range(cols // TILE):
            tile = slice(t * TILE, (t + 1) * TILE)
            d_upper, d_rest = split(rows_ref[start + row : start + row + PIECE, tile])
            both = jnp.dot(stack, d_upper, preferred_element_type=f32)
            value = both[:width] + both[width:] + jnp.dot(upper, d_rest, preferred_element_type=f32)
            if row > 0:
                value += total[:, tile]
            elif before:
                value += old[:, tile]
            total[:, tile] = value
    if slices:
        step = total.shape[0] // slices
        for place in range(slices):
            at = pl.multiple_of((place ^ own_ref[1]) * step, step)
            group, row = ((0, 0), (1, 0), (1, step), (0, step))[place // 2]
            outs[2 * (place % 2) + group][row : row + step] = total[pl.ds(at, step)]


def project(own, rows, part, before=None, slices=0, start=0):
    cols = rows.shape[1]
    width = part.shape[1]
    args = [own, rows, part] + ([] if before is None else [before])
    if slices:
        out = [jax.ShapeDtypeStruct((width // 4, cols), f32)] * 4
    else:
        out = [jax.ShapeDtypeStruct((width, cols), f32)]
    return pl.pallas_call(
        functools.partial(project_kernel, start, before is not None, slices),
        in_specs=[SMEM] + [VMEM] * (len(args) - 1),
        out_specs=[VMEM] * len(out),
        out_shape=out,
        scratch_shapes=[pltpu.VMEM((width, cols), f32)] if slices else [],
        compiler_params=params(),
        cost_estimate=cost(6 * part.shape[0] / rows.shape[0]),
        name="project",
    )(*args)


def factor_kernel(index, count, in_ref, out_ref, *scratch):
    n = in_ref.shape[0]
    last = index == count - 1
    work = scratch[0] if last else out_ref
    if index == 0:
        row = lax.broadcasted_iota(jnp.int32, (n, n), 0)
        col = lax.broadcasted_iota(jnp.int32, (n, n), 1)
        work[:, :n] = in_ref[...]
        work[:, n:] = jnp.where(row == col, 1.0, 0.0).astype(f32)
    else:
        work[...] = in_ref[...]
    sub = lax.broadcasted_iota(jnp.int32, (8, n), 0)
    panels = n // 8
    for b in range(panels * index // count, panels * (index + 1) // count):
        top = slice(8 * b, 8 * b + 8)
        panel = work[top, :]
        spread = [jnp.broadcast_to(panel[:, 8 * b + j : 8 * b + j + 1], (8, n)) for j in range(8)]
        e = [
            [jnp.broadcast_to(spread[j][i : i + 1, :], (8, n)) for j in range(i + 1)]
            for i in range(8)
        ]
        left = [jnp.broadcast_to(panel[i : i + 1, :n], (8, n)) for i in range(8)]
        right = [jnp.broadcast_to(panel[i : i + 1, n:], (8, n)) for i in range(8)]
        for j in range(8):
            scale = lax.rsqrt(e[j][j])
            left[j] = left[j] * scale
            right[j] = right[j] * scale
            low = {i: e[i][j] * scale for i in range(j + 1, 8)}
            for i in range(j + 1, 8):
                for k in range(j + 1, i + 1):
                    e[i][k] = e[i][k] - low[i] * low[k]
                left[i] = left[i] - low[i] * left[j]
                right[i] = right[i] - low[i] * right[j]
        l_panel, r_panel = left[0], right[0]
        for i in range(1, 8):
            l_panel = jnp.where(sub == i, left[i], l_panel)
            r_panel = jnp.where(sub == i, right[i], r_panel)
        work[top, n:] = r_panel
        if b < panels - 1:
            rows = slice(8 * b + 8, 8 * b + 16)
            l_next, r_next = work[rows, :n], work[rows, n:]
            column = l_panel.T[rows, :]
            for j in range(8):
                factors = jnp.broadcast_to(column[:, j : j + 1], (8, n))
                l_next = l_next - factors * left[j]
                r_next = r_next - factors * right[j]
            work[rows, :n] = l_next
            work[rows, n:] = r_next
        if b < panels - 2:
            done = jnp.concatenate([l_panel, r_panel], 1)
            change = dot(l_panel, done, 0, 0)
            below = slice(8 * b + 16, n)
            work[below, :] = work[below, :] - change[8 * b + 16 :, :]
    if last:
        out_ref[...] = work[:, n:]


def factor(index, count, value):
    n = value.shape[0]
    last = index == count - 1
    return pl.pallas_call(
        functools.partial(factor_kernel, index, count),
        in_specs=[VMEM],
        out_specs=VMEM,
        out_shape=jax.ShapeDtypeStruct((n, n if last else 2 * n), f32),
        scratch_shapes=[pltpu.VMEM((n, 2 * n), f32)] if last else [],
        compiler_params=params(),
        cost_estimate=cost(0.01),
        name="factor",
    )(value)


def finish_kernel(own_ref, inverse_ref, *refs):
    parts, (out_ref, gram_ref, total) = refs[:-3], refs[-3:]
    step = total.shape[0] // SLICES
    for place in range(SLICES):
        at = pl.multiple_of((place ^ own_ref[1]) * step, step)
        group, row = (1, place // 2 * step - step) if place > 1 else (0, 0)
        total[pl.ds(at, step)] = parts[2 * (place % 2) + group][row : row + step]
    upper, rest = split(inverse_ref[...])
    stack = jnp.concatenate([upper, rest], 0)
    width = upper.shape[0]
    gram = jnp.zeros((2 * width, width), f32)
    for t in range(total.shape[1] // TILE):
        tile = slice(t * TILE, (t + 1) * TILE)
        t_upper, t_rest = split(total[:, tile])
        both = jnp.dot(stack, t_upper, preferred_element_type=f32)
        value = both[:width] + both[width:] + jnp.dot(upper, t_rest, preferred_element_type=f32)
        out_ref[:, tile] = value
        v_upper, v_rest = split(value)
        gram += lax.dot_general(
            jnp.concatenate([v_upper, v_rest], 0),
            v_upper,
            (((1,), (1,)), ((), ())),
            preferred_element_type=f32,
        )
    cross = gram[width:]
    gram_ref[...] = gram[:width] + (cross + cross.T)


def finish(own, inverse, parts):
    width = inverse.shape[0]
    cols = parts[0].shape[1]
    return pl.pallas_call(
        finish_kernel,
        in_specs=[SMEM] + [VMEM] * (1 + len(parts)),
        out_specs=[VMEM] * 2,
        out_shape=[
            jax.ShapeDtypeStruct((width, cols), f32),
            jax.ShapeDtypeStruct((width, width), f32),
        ],
        scratch_shapes=[pltpu.VMEM((width, cols), f32)],
        compiler_params=params(),
        cost_estimate=cost(8),
        name="finish",
    )(own, inverse, *parts)


def per_device(data, omega):
    nrow, ncol = lax.axis_size("row"), lax.axis_size("col")
    quarter = data.shape[0] // ncol
    assert ncol == 4 and quarter == 2 * PIECE and nrow >= 8
    total_rows = data.shape[0] * nrow
    own = jnp.stack([lax.axis_index("col"), lax.axis_index("row") % 8]).astype(jnp.int32)
    bits = [1 << k for k in range(nrow.bit_length() - 1)]

    data = pltpu.with_memory_space_constraint(data, pltpu.HBM)
    omega = pltpu.with_memory_space_constraint(omega, pltpu.HBM)

    part, rows3, rows2, wide = sketch(own, data, omega, (3,), (2,), True)
    pair, wide = fence((sketch_held(rows2, wide) + swap(part, "col", 1), wide))
    away = swap(pair, "col", 2)
    part, here, rows1, rows0 = sketch(own, data, wide, (1, 0))
    part_a, part_b, away = fence((swap(part[:PIECE], "col", 1), swap(part[PIECE:], "col", 1), away))
    sketched = here + jnp.concatenate([part_a, part_b], 0) + away

    third = swap(sketched, "col", 2)
    second = swap(sketched, "col", 1)
    gram = dot(sketched, sketched, 0, 0)
    far = swap(gram, "row", bits[0])
    (acc,) = project(own, rows0, sketched)
    far, acc, second = fence((far, acc, second))
    gram = gram + far
    far = swap(gram, "row", bits[1])
    (acc,) = project(own, rows1, second, acc)
    far, acc = fence((far, acc))
    gram = gram + far
    far = swap(gram, "row", bits[2])
    third, acc, far = fence((third, acc, far))
    gram = gram + far
    for bit in bits[3:]:
        gram = gram + swap(gram, "row", bit)
    fourth = swap(third, "col", 1)
    (acc,) = project(own, rows2, third, acc)
    fourth, acc = fence((fourth, acc))
    far = swap(gram, "col", 1)
    outer_keep, inner_keep, outer_send, inner_send = project(own, rows3, fourth, acc, SLICES)
    far, outer_keep, inner_keep, outer_send, inner_send = fence(
        (far, outer_keep, inner_keep, outer_send, inner_send)
    )
    gram = gram + far

    step = outer_keep.shape[0] // 2
    outer_got, state = fence((swap(outer_send, "row", 1), gram + swap(gram, "col", 2)))
    zero, six = outer_keep[:step] + outer_got[:step], outer_keep[step:] + outer_got[step:]
    zero, six, state = fence((zero, six, state))
    six = swap(six, "row", 6)
    inner_got = swap(inner_send, "row", 1)
    two, four = inner_keep[:step] + inner_got[:step], inner_keep[step:] + inner_got[step:]
    four, two = swap(four, "row", 4), swap(two, "row", 2)
    six, four, two, state = fence((six, four, two, factor(0, 3, state)))
    zero = (zero + two) + (four + six)
    for bit in bits[3:]:
        zero = zero + swap(zero, "row", bit)
    zero, state = fence((zero, state))
    got = [swap(zero, "row", q) for q in (2, 4, 6, 1)]
    *got, state = fence((*got, factor(1, 3, state)))
    others, state = fence((jnp.concatenate(got[:3], 0), state))
    far, inverse = fence((swap(others, "row", 1), factor(2, 3, state)))
    projected, small = finish(own, inverse, [zero, others, got[3], far])

    across = [swap(small, "col", bit) for bit in (2, 3, 1)]
    *across, basis = fence((*across, dot(sketched, inverse, 1, 1)))
    small = (small + across[2]) + (across[0] + across[1])
    return (basis, projected, small / total_rows)


def solution(mesh):
    placed = (P("row", "col"), P("col", None))
    return jax.shard_map(
        per_device,
        mesh=mesh,
        in_specs=placed,
        out_specs=(P(("row", "col"), None), P(None, "col"), P()),
        check_vma=False,
    )
```

```python
import functools

import jax
import jax.numpy as jnp
from jax import lax
from jax.experimental import pallas as pl
from jax.experimental.pallas import tpu as pltpu
from jax.sharding import PartitionSpec as P

full = lax.Precision.HIGHEST
f32 = jnp.float32
bf16 = jnp.bfloat16

PIECE = 512
TILE = 256
RUN = 512
SLICES = 8
SMEM = pl.BlockSpec(memory_space=pltpu.SMEM)
VMEM = pl.BlockSpec(memory_space=pltpu.VMEM)
HBM = pl.BlockSpec(memory_space=pltpu.HBM)
fence = lax.optimization_barrier


def cost(mib):
    return pl.CostEstimate(flops=1, bytes_accessed=int(mib * 2**20), transcendentals=0)


def params():
    return pltpu.CompilerParams(vmem_limit_bytes=16 * 1024 * 1024)


def swap(value, axis, bit):
    return lax.ppermute(value, axis, [(i, i ^ bit) for i in range(lax.axis_size(axis))])


def dot(a, b, a_dim, b_dim, precision=full):
    return lax.dot_general(
        a, b, (((a_dim,), (b_dim,)), ((), ())), precision=precision, preferred_element_type=f32
    )


def split(value):
    upper = value.astype(bf16)
    return upper, (value - upper.astype(f32)).astype(bf16)


def multiply(held, wide, out):
    quarter, cols = held.shape
    width = out.shape[1]
    for row in range(0, quarter, PIECE):
        yield row
        for t in range(cols // TILE):
            tile = slice(t * TILE, (t + 1) * TILE)
            upper, rest = split(held[row : row + PIECE, tile])
            one = jnp.dot(upper, wide[tile, :], preferred_element_type=f32)
            two = jnp.dot(rest, wide[tile, :width], preferred_element_type=f32)
            both, more = (one, two) if t == 0 else (both + one, more + two)
        out[row : row + PIECE] = both[:, :width] + both[:, width:] + more


def sketch_kernel(places, ahead, first, own_ref, data_ref, omega_ref, *refs):
    count, total = len(places), len(places) + len(ahead)
    if first:
        refs, (omega_held, omega_sem) = refs[:-2], refs[-2:]
        omega_copy = pltpu.make_async_copy(omega_ref, omega_held, omega_sem)
        omega_copy.start()
    outs, held, sems = refs[:count], refs[count : count + total], refs[-1]
    quarter = held[0].shape[0]
    copies = {}
    for k, place in enumerate(places + ahead):
        for row in range(0, quarter, RUN):
            at = pl.multiple_of((own_ref[0] ^ place) * quarter + row, RUN)
            copy = pltpu.make_async_copy(
                data_ref.at[pl.ds(at, RUN)], held[k].at[pl.ds(row, RUN)], sems.at[k, row // RUN]
            )
            copy.start()
            copies[k, row] = copy
    if first:
        width = omega_ref.shape[1]
        wide = refs[count + total]
        omega_copy.wait()
        upper, rest = split(omega_held[...])
        wide[:, :width] = upper
        wide[:, width:] = rest
    else:
        wide = omega_ref
    for k in range(count):
        for row in multiply(held[k], wide, outs[k]):
            for run in range(row, row + PIECE, RUN):
                copies[k, run].wait()
    for k in range(count, total):
        for row in range(0, quarter, RUN):
            copies[k, row].wait()


def sketch(own, data, omega, places, ahead=(), first=False):
    cols = data.shape[1]
    width = omega.shape[1] if first else omega.shape[1] // 2
    quarter = data.shape[0] // lax.axis_size("col")
    total = len(places) + len(ahead)
    out = [jax.ShapeDtypeStruct((quarter, width), f32)] * len(places)
    out += [pltpu.VMEM((quarter, cols), f32)] * total
    scratch = [pltpu.SemaphoreType.DMA((total, quarter // RUN))]
    if first:
        out.append(jax.ShapeDtypeStruct((cols, 2 * width), bf16))
        scratch += [pltpu.VMEM(omega.shape, f32), pltpu.SemaphoreType.DMA]
    return pl.pallas_call(
        functools.partial(sketch_kernel, places, ahead, first),
        in_specs=[SMEM, HBM, HBM if first else VMEM],
        out_specs=[VMEM] * len(out),
        out_shape=out,
        scratch_shapes=scratch,
        compiler_params=params(),
        cost_estimate=cost(0.01),
        name="partial_sketch",
    )(own, data, omega)


def held_kernel(rows_ref, wide_ref, out_ref):
    for _ in multiply(rows_ref, wide_ref, out_ref):
        pass


def sketch_held(rows, wide):
    return pl.pallas_call(
        held_kernel,
        in_specs=[VMEM] * 2,
        out_specs=VMEM,
        out_shape=jax.ShapeDtypeStruct((rows.shape[0], wide.shape[1] // 2), f32),
        compiler_params=params(),
        cost_estimate=cost(0.01),
        name="partial_sketch_held",
    )(rows, wide)


def project_kernel(before, slices, own_ref, rows_ref, part_ref, *refs):
    old, refs = (refs[0], refs[1:]) if before else (None, refs)
    outs, total = (refs[:-1], refs[-1]) if slices else (refs, refs[0])
    upper, rest = split(part_ref[...].T)
    stack = jnp.concatenate([upper, rest], 0)
    width = upper.shape[0]
    for t in range(rows_ref.shape[1] // TILE):
        tile = slice(t * TILE, (t + 1) * TILE)
        d_upper, d_rest = split(rows_ref[:, tile])
        both = jnp.dot(stack, d_upper, preferred_element_type=f32)
        value = both[:width] + both[width:] + jnp.dot(upper, d_rest, preferred_element_type=f32)
        total[:, tile] = value + old[:, tile] if before else value
    if slices:
        step = total.shape[0] // slices
        for place in range(slices):
            at = pl.multiple_of((place ^ own_ref[1]) * step, step)
            group, row = ((0, 0), (1, 0), (1, step), (0, step))[place // 2]
            outs[2 * (place % 2) + group][row : row + step] = total[pl.ds(at, step)]


def project(own, rows, part, before=None, slices=0):
    cols = rows.shape[1]
    width = part.shape[1]
    args = [own, rows, part] + ([] if before is None else [before])
    if slices:
        out = [jax.ShapeDtypeStruct((width // 4, cols), f32)] * 4
    else:
        out = [jax.ShapeDtypeStruct((width, cols), f32)]
    return pl.pallas_call(
        functools.partial(project_kernel, before is not None, slices),
        in_specs=[SMEM] + [VMEM] * (len(args) - 1),
        out_specs=[VMEM] * len(out),
        out_shape=out,
        scratch_shapes=[pltpu.VMEM((width, cols), f32)] if slices else [],
        compiler_params=params(),
        cost_estimate=cost(6),
        name="project",
    )(*args)


def factor_kernel(first, end, in_ref, out_ref, *scratch):
    n = in_ref.shape[0]
    panels = n // 8
    last = end == panels
    work = scratch[0] if last else out_ref
    if first == 0:
        row = lax.broadcasted_iota(jnp.int32, (n, n), 0)
        col = lax.broadcasted_iota(jnp.int32, (n, n), 1)
        work[:, :n] = in_ref[...]
        work[:, n:] = jnp.where(row == col, 1.0, 0.0).astype(f32)
    else:
        work[...] = in_ref[...]
    sub = lax.broadcasted_iota(jnp.int32, (8, n), 0)
    for b in range(first, end):
        top = slice(8 * b, 8 * b + 8)
        panel = work[top, :]
        spread = [jnp.broadcast_to(panel[:, 8 * b + j : 8 * b + j + 1], (8, n)) for j in range(8)]
        e = [
            [jnp.broadcast_to(spread[j][i : i + 1, :], (8, n)) for j in range(i + 1)]
            for i in range(8)
        ]
        left = [jnp.broadcast_to(panel[i : i + 1, :n], (8, n)) for i in range(8)]
        right = [jnp.broadcast_to(panel[i : i + 1, n:], (8, n)) for i in range(8)]
        for j in range(8):
            scale = lax.rsqrt(e[j][j])
            left[j] = left[j] * scale
            right[j] = right[j] * scale
            low = {i: e[i][j] * scale for i in range(j + 1, 8)}
            for i in range(j + 1, 8):
                for k in range(j + 1, i + 1):
                    e[i][k] = e[i][k] - low[i] * low[k]
                left[i] = left[i] - low[i] * left[j]
                right[i] = right[i] - low[i] * right[j]
        l_panel, r_panel = left[0], right[0]
        for i in range(1, 8):
            l_panel = jnp.where(sub == i, left[i], l_panel)
            r_panel = jnp.where(sub == i, right[i], r_panel)
        work[top, n:] = r_panel
        if b < panels - 1:
            rows = slice(8 * b + 8, 8 * b + 16)
            l_next, r_next = work[rows, :n], work[rows, n:]
            column = l_panel.T[rows, :]
            for j in range(8):
                factors = jnp.broadcast_to(column[:, j : j + 1], (8, n))
                l_next = l_next - factors * left[j]
                r_next = r_next - factors * right[j]
            work[rows, :n] = l_next
            work[rows, n:] = r_next
        if b < panels - 2:
            done = jnp.concatenate([l_panel, r_panel], 1)
            change = dot(l_panel, done, 0, 0)
            below = slice(8 * b + 16, n)
            work[below, :] = work[below, :] - change[8 * b + 16 :, :]
    if last:
        out_ref[...] = work[:, n:]


def factor(first, end, value):
    n = value.shape[0]
    last = end == n // 8
    return pl.pallas_call(
        functools.partial(factor_kernel, first, end),
        in_specs=[VMEM],
        out_specs=VMEM,
        out_shape=jax.ShapeDtypeStruct((n, n if last else 2 * n), f32),
        scratch_shapes=[pltpu.VMEM((n, 2 * n), f32)] if last else [],
        compiler_params=params(),
        cost_estimate=cost(0.01),
        name="factor",
    )(value)


def finish_kernel(own_ref, inverse_ref, *refs):
    parts, (out_ref, gram_ref, total) = refs[:-3], refs[-3:]
    step = total.shape[0] // SLICES
    for place in range(SLICES):
        at = pl.multiple_of((place ^ own_ref[1]) * step, step)
        group, row = (1, place // 2 * step - step) if place > 1 else (0, 0)
        total[pl.ds(at, step)] = parts[2 * (place % 2) + group][row : row + step]
    upper, rest = split(inverse_ref[...])
    stack = jnp.concatenate([upper, rest], 0)
    width = upper.shape[0]
    gram = jnp.zeros((2 * width, width), f32)
    for t in range(total.shape[1] // TILE):
        tile = slice(t * TILE, (t + 1) * TILE)
        t_upper, t_rest = split(total[:, tile])
        both = jnp.dot(stack, t_upper, preferred_element_type=f32)
        value = both[:width] + both[width:] + jnp.dot(upper, t_rest, preferred_element_type=f32)
        out_ref[:, tile] = value
        v_upper, v_rest = split(value)
        gram += lax.dot_general(
            jnp.concatenate([v_upper, v_rest], 0),
            v_upper,
            (((1,), (1,)), ((), ())),
            preferred_element_type=f32,
        )
    cross = gram[width:]
    gram_ref[...] = gram[:width] + (cross + cross.T)


def finish(own, inverse, parts):
    width = inverse.shape[0]
    cols = parts[0].shape[1]
    return pl.pallas_call(
        finish_kernel,
        in_specs=[SMEM] + [VMEM] * (1 + len(parts)),
        out_specs=[VMEM] * 2,
        out_shape=[
            jax.ShapeDtypeStruct((width, cols), f32),
            jax.ShapeDtypeStruct((width, width), f32),
        ],
        scratch_shapes=[pltpu.VMEM((width, cols), f32)],
        compiler_params=params(),
        cost_estimate=cost(8),
        name="finish",
    )(own, inverse, *parts)


def per_device(data, omega):
    nrow, ncol = lax.axis_size("row"), lax.axis_size("col")
    quarter = data.shape[0] // ncol
    assert ncol == 4 and quarter == 2 * PIECE and nrow >= 8
    total_rows = data.shape[0] * nrow
    own = jnp.stack([lax.axis_index("col"), lax.axis_index("row") % 8]).astype(jnp.int32)
    bits = [1 << k for k in range(nrow.bit_length() - 1)]

    data = pltpu.with_memory_space_constraint(data, pltpu.HBM)
    omega = pltpu.with_memory_space_constraint(omega, pltpu.HBM)

    part, rows3, rows2, wide = sketch(own, data, omega, (3,), (2,), True)
    pair, wide = fence((sketch_held(rows2, wide) + swap(part, "col", 1), wide))
    away = swap(pair, "col", 2)
    part, here, rows1, rows0 = sketch(own, data, wide, (1, 0))
    part_a, part_b, away = fence((swap(part[:PIECE], "col", 1), swap(part[PIECE:], "col", 1), away))
    sketched = here + jnp.concatenate([part_a, part_b], 0) + away

    third = swap(sketched, "col", 2)
    second = swap(sketched, "col", 1)
    gram = dot(sketched, sketched, 0, 0)
    far = swap(gram, "row", bits[0])
    (acc,) = project(own, rows0, sketched)
    far, acc, second = fence((far, acc, second))
    gram = gram + far
    far = swap(gram, "row", bits[1])
    (acc,) = project(own, rows1, second, acc)
    far, acc = fence((far, acc))
    gram = gram + far
    far = swap(gram, "col", 1)
    far, acc, third = fence((far, acc, third))
    gram = gram + far
    fourth = swap(third, "col", 1)
    (acc,) = project(own, rows2, third, acc)
    fourth, acc = fence((fourth, acc))
    outer_keep, inner_keep, outer_send, inner_send = project(own, rows3, fourth, acc, SLICES)
    gram, outer_keep, inner_keep, outer_send, inner_send = fence(
        (gram, outer_keep, inner_keep, outer_send, inner_send)
    )

    step = outer_keep.shape[0] // 2
    outer_got = swap(outer_send, "row", 1)
    zero, six = outer_keep[:step] + outer_got[:step], outer_keep[step:] + outer_got[step:]
    zero, six = fence((zero, six))
    six = swap(six, "row", 6)
    inner_got, far = fence((swap(inner_send, "row", 1), swap(gram, "row", bits[2])))
    gram = gram + far
    two, four = inner_keep[:step] + inner_got[:step], inner_keep[step:] + inner_got[step:]
    four, two = swap(four, "row", 4), swap(two, "row", 2)
    for bit in bits[3:]:
        gram = gram + swap(gram, "row", bit)
    six, four, two, far = fence((six, four, two, swap(gram, "col", 2)))
    state = gram + far
    zero = (zero + two) + (four + six)
    for bit in bits[3:]:
        zero = zero + swap(zero, "row", bit)
    zero, state = fence((zero, state))
    got = [swap(zero, "row", q) for q in (2, 4, 6, 1)]
    *got, state = fence((*got, factor(0, 6, state)))
    others, state = fence((jnp.concatenate(got[:3], 0), state))
    far, inverse = fence((swap(others, "row", 1), factor(6, 16, state)))
    projected, small = finish(own, inverse, [zero, others, got[3], far])

    across = [swap(small, "col", bit) for bit in (2, 3, 1)]
    *across, basis = fence((*across, dot(sketched, inverse, 1, 1)))
    small = (small + across[2]) + (across[0] + across[1])
    return (basis, projected, small / total_rows)


def solution(mesh):
    placed = (P("row", "col"), P("col", None))
    return jax.shard_map(
        per_device,
        mesh=mesh,
        in_specs=placed,
        out_specs=(P(("row", "col"), None), P(None, "col"), P()),
        check_vma=False,
    )
```

```python
import functools

import jax
import jax.numpy as jnp
from jax import lax
from jax.experimental import pallas as pl
from jax.experimental.pallas import tpu as pltpu
from jax.sharding import PartitionSpec as P

full = lax.Precision.HIGHEST
f32 = jnp.float32
bf16 = jnp.bfloat16

PIECE = 512
TILE = 256
RUN = 512
SLICES = 8
SMEM = pl.BlockSpec(memory_space=pltpu.SMEM)
VMEM = pl.BlockSpec(memory_space=pltpu.VMEM)
HBM = pl.BlockSpec(memory_space=pltpu.HBM)
fence = lax.optimization_barrier


def cost(mib):
    return pl.CostEstimate(flops=1, bytes_accessed=int(mib * 2**20), transcendentals=0)


def params():
    return pltpu.CompilerParams(vmem_limit_bytes=16 * 1024 * 1024)


def swap(value, axis, bit):
    return lax.ppermute(value, axis, [(i, i ^ bit) for i in range(lax.axis_size(axis))])


def dot(a, b, a_dim, b_dim, precision=full):
    return lax.dot_general(
        a, b, (((a_dim,), (b_dim,)), ((), ())), precision=precision, preferred_element_type=f32
    )


def split(value):
    upper = value.astype(bf16)
    return upper, (value - upper.astype(f32)).astype(bf16)


def multiply(held, wide, out):
    quarter, cols = held.shape
    width = out.shape[1]
    for row in range(0, quarter, PIECE):
        yield row
        for t in range(cols // TILE):
            tile = slice(t * TILE, (t + 1) * TILE)
            upper, rest = split(held[row : row + PIECE, tile])
            one = jnp.dot(upper, wide[tile, :], preferred_element_type=f32)
            two = jnp.dot(rest, wide[tile, :width], preferred_element_type=f32)
            both, more = (one, two) if t == 0 else (both + one, more + two)
        out[row : row + PIECE] = both[:, :width] + both[:, width:] + more


def sketch_kernel(places, ahead, first, own_ref, data_ref, omega_ref, *refs):
    count, total = len(places), len(places) + len(ahead)
    if first:
        refs, (omega_held, omega_sem) = refs[:-2], refs[-2:]
        omega_copy = pltpu.make_async_copy(omega_ref, omega_held, omega_sem)
        omega_copy.start()
    outs, held, sems = refs[:count], refs[count : count + total], refs[-1]
    quarter = held[0].shape[0]
    copies = {}
    for k, place in enumerate(places + ahead):
        for row in range(0, quarter, RUN):
            at = pl.multiple_of((own_ref[0] ^ place) * quarter + row, RUN)
            copy = pltpu.make_async_copy(
                data_ref.at[pl.ds(at, RUN)], held[k].at[pl.ds(row, RUN)], sems.at[k, row // RUN]
            )
            copy.start()
            copies[k, row] = copy
    if first:
        width = omega_ref.shape[1]
        wide = refs[count + total]
        omega_copy.wait()
        upper, rest = split(omega_held[...])
        wide[:, :width] = upper
        wide[:, width:] = rest
    else:
        wide = omega_ref
    for k in range(count):
        for row in multiply(held[k], wide, outs[k]):
            for run in range(row, row + PIECE, RUN):
                copies[k, run].wait()
    for k in range(count, total):
        for row in range(0, quarter, RUN):
            copies[k, row].wait()


def sketch(own, data, omega, places, ahead=(), first=False):
    cols = data.shape[1]
    width = omega.shape[1] if first else omega.shape[1] // 2
    quarter = data.shape[0] // lax.axis_size("col")
    total = len(places) + len(ahead)
    out = [jax.ShapeDtypeStruct((quarter, width), f32)] * len(places)
    out += [pltpu.VMEM((quarter, cols), f32)] * total
    scratch = [pltpu.SemaphoreType.DMA((total, quarter // RUN))]
    if first:
        out.append(jax.ShapeDtypeStruct((cols, 2 * width), bf16))
        scratch += [pltpu.VMEM(omega.shape, f32), pltpu.SemaphoreType.DMA]
    return pl.pallas_call(
        functools.partial(sketch_kernel, places, ahead, first),
        in_specs=[SMEM, HBM, HBM if first else VMEM],
        out_specs=[VMEM] * len(out),
        out_shape=out,
        scratch_shapes=scratch,
        compiler_params=params(),
        cost_estimate=cost(0.01),
        name="partial_sketch",
    )(own, data, omega)


def held_kernel(rows_ref, wide_ref, out_ref):
    for _ in multiply(rows_ref, wide_ref, out_ref):
        pass


def sketch_held(rows, wide):
    return pl.pallas_call(
        held_kernel,
        in_specs=[VMEM] * 2,
        out_specs=VMEM,
        out_shape=jax.ShapeDtypeStruct((rows.shape[0], wide.shape[1] // 2), f32),
        compiler_params=params(),
        cost_estimate=cost(0.01),
        name="partial_sketch_held",
    )(rows, wide)


def project_kernel(before, slices, own_ref, rows_ref, part_ref, *refs):
    old, refs = (refs[0], refs[1:]) if before else (None, refs)
    outs, total = (refs[:-1], refs[-1]) if slices else (refs, refs[0])
    upper, rest = split(part_ref[...].T)
    stack = jnp.concatenate([upper, rest], 0)
    width = upper.shape[0]
    for t in range(rows_ref.shape[1] // TILE):
        tile = slice(t * TILE, (t + 1) * TILE)
        d_upper, d_rest = split(rows_ref[:, tile])
        both = jnp.dot(stack, d_upper, preferred_element_type=f32)
        value = both[:width] + both[width:] + jnp.dot(upper, d_rest, preferred_element_type=f32)
        total[:, tile] = value + old[:, tile] if before else value
    if slices:
        step = total.shape[0] // slices
        for place in range(slices):
            at = pl.multiple_of((place ^ own_ref[1]) * step, step)
            group, row = ((0, 0), (1, 0), (1, step), (0, step))[place // 2]
            outs[2 * (place % 2) + group][row : row + step] = total[pl.ds(at, step)]


def project(own, rows, part, before=None, slices=0):
    cols = rows.shape[1]
    width = part.shape[1]
    args = [own, rows, part] + ([] if before is None else [before])
    if slices:
        out = [jax.ShapeDtypeStruct((width // 4, cols), f32)] * 4
    else:
        out = [jax.ShapeDtypeStruct((width, cols), f32)]
    return pl.pallas_call(
        functools.partial(project_kernel, before is not None, slices),
        in_specs=[SMEM] + [VMEM] * (len(args) - 1),
        out_specs=[VMEM] * len(out),
        out_shape=out,
        scratch_shapes=[pltpu.VMEM((width, cols), f32)] if slices else [],
        compiler_params=params(),
        cost_estimate=cost(6),
        name="project",
    )(*args)


def factor_kernel(first, end, in_ref, out_ref, *scratch):
    n = in_ref.shape[0]
    panels = n // 8
    last = end == panels
    work = scratch[0] if last else out_ref
    if first == 0:
        row = lax.broadcasted_iota(jnp.int32, (n, n), 0)
        col = lax.broadcasted_iota(jnp.int32, (n, n), 1)
        work[:, :n] = in_ref[...]
        work[:, n:] = jnp.where(row == col, 1.0, 0.0).astype(f32)
    else:
        work[...] = in_ref[...]
    sub = lax.broadcasted_iota(jnp.int32, (8, n), 0)
    for b in range(first, end):
        top = slice(8 * b, 8 * b + 8)
        panel = work[top, :]
        spread = [jnp.broadcast_to(panel[:, 8 * b + j : 8 * b + j + 1], (8, n)) for j in range(8)]
        e = [
            [jnp.broadcast_to(spread[j][i : i + 1, :], (8, n)) for j in range(i + 1)]
            for i in range(8)
        ]
        left = [jnp.broadcast_to(panel[i : i + 1, :n], (8, n)) for i in range(8)]
        right = [jnp.broadcast_to(panel[i : i + 1, n:], (8, n)) for i in range(8)]
        for j in range(8):
            scale = lax.rsqrt(e[j][j])
            left[j] = left[j] * scale
            right[j] = right[j] * scale
            low = {i: e[i][j] * scale for i in range(j + 1, 8)}
            for i in range(j + 1, 8):
                for k in range(j + 1, i + 1):
                    e[i][k] = e[i][k] - low[i] * low[k]
                left[i] = left[i] - low[i] * left[j]
                right[i] = right[i] - low[i] * right[j]
        l_panel, r_panel = left[0], right[0]
        for i in range(1, 8):
            l_panel = jnp.where(sub == i, left[i], l_panel)
            r_panel = jnp.where(sub == i, right[i], r_panel)
        work[top, n:] = r_panel
        if b < panels - 1:
            rows = slice(8 * b + 8, 8 * b + 16)
            l_next, r_next = work[rows, :n], work[rows, n:]
            column = l_panel.T[rows, :]
            for j in range(8):
                factors = jnp.broadcast_to(column[:, j : j + 1], (8, n))
                l_next = l_next - factors * left[j]
                r_next = r_next - factors * right[j]
            work[rows, :n] = l_next
            work[rows, n:] = r_next
        if b < panels - 2:
            done = jnp.concatenate([l_panel, r_panel], 1)
            change = dot(l_panel, done, 0, 0)
            below = slice(8 * b + 16, n)
            work[below, :] = work[below, :] - change[8 * b + 16 :, :]
    if last:
        out_ref[...] = work[:, n:]


def factor(first, end, value):
    n = value.shape[0]
    last = end == n // 8
    return pl.pallas_call(
        functools.partial(factor_kernel, first, end),
        in_specs=[VMEM],
        out_specs=VMEM,
        out_shape=jax.ShapeDtypeStruct((n, n if last else 2 * n), f32),
        scratch_shapes=[pltpu.VMEM((n, 2 * n), f32)] if last else [],
        compiler_params=params(),
        cost_estimate=cost(0.01),
        name="factor",
    )(value)


def finish_kernel(own_ref, inverse_ref, *refs):
    parts, (out_ref, gram_ref, total) = refs[:-3], refs[-3:]
    step = total.shape[0] // SLICES
    for place in range(SLICES):
        at = pl.multiple_of((place ^ own_ref[1]) * step, step)
        group, row = (1, place // 2 * step - step) if place > 1 else (0, 0)
        total[pl.ds(at, step)] = parts[2 * (place % 2) + group][row : row + step]
    upper, rest = split(inverse_ref[...])
    stack = jnp.concatenate([upper, rest], 0)
    width = upper.shape[0]
    gram = jnp.zeros((2 * width, width), f32)
    for t in range(total.shape[1] // TILE):
        tile = slice(t * TILE, (t + 1) * TILE)
        t_upper, t_rest = split(total[:, tile])
        both = jnp.dot(stack, t_upper, preferred_element_type=f32)
        value = both[:width] + both[width:] + jnp.dot(upper, t_rest, preferred_element_type=f32)
        out_ref[:, tile] = value
        v_upper, v_rest = split(value)
        gram += lax.dot_general(
            jnp.concatenate([v_upper, v_rest], 0),
            v_upper,
            (((1,), (1,)), ((), ())),
            preferred_element_type=f32,
        )
    cross = gram[width:]
    gram_ref[...] = gram[:width] + (cross + cross.T)


def finish(own, inverse, parts):
    width = inverse.shape[0]
    cols = parts[0].shape[1]
    return pl.pallas_call(
        finish_kernel,
        in_specs=[SMEM] + [VMEM] * (1 + len(parts)),
        out_specs=[VMEM] * 2,
        out_shape=[pltpu.VMEM((width, cols), f32), jax.ShapeDtypeStruct((width, width), f32)],
        scratch_shapes=[pltpu.VMEM((width, cols), f32)],
        compiler_params=params(),
        cost_estimate=cost(8),
        name="finish",
    )(own, inverse, *parts)


def per_device(data, omega):
    nrow, ncol = lax.axis_size("row"), lax.axis_size("col")
    quarter = data.shape[0] // ncol
    assert ncol == 4 and quarter == 2 * PIECE and nrow >= 8
    total_rows = data.shape[0] * nrow
    own = jnp.stack([lax.axis_index("col"), lax.axis_index("row") % 8]).astype(jnp.int32)
    bits = [1 << k for k in range(nrow.bit_length() - 1)]

    data = pltpu.with_memory_space_constraint(data, pltpu.HBM)
    omega = pltpu.with_memory_space_constraint(omega, pltpu.HBM)

    part, rows3, rows2, wide = sketch(own, data, omega, (3,), (2,), True)
    pair, wide = fence((sketch_held(rows2, wide) + swap(part, "col", 1), wide))
    away = swap(pair, "col", 2)
    part, here, rows1, rows0 = sketch(own, data, wide, (1, 0))
    part_a, part_b, away = fence((swap(part[:PIECE], "col", 1), swap(part[PIECE:], "col", 1), away))
    sketched = here + jnp.concatenate([part_a, part_b], 0) + away

    third = swap(sketched, "col", 2)
    second = swap(sketched, "col", 1)
    gram = dot(sketched, sketched, 0, 0)
    far = swap(gram, "row", bits[0])
    (acc,) = project(own, rows0, sketched)
    far, acc, second = fence((far, acc, second))
    gram = gram + far
    far = swap(gram, "row", bits[1])
    (acc,) = project(own, rows1, second, acc)
    far, acc = fence((far, acc))
    gram = gram + far
    far = swap(gram, "col", 1)
    far, acc, third = fence((far, acc, third))
    gram = gram + far
    fourth = swap(third, "col", 1)
    (acc,) = project(own, rows2, third, acc)
    fourth, acc = fence((fourth, acc))
    outer_keep, inner_keep, outer_send, inner_send = project(own, rows3, fourth, acc, SLICES)
    gram, outer_keep, inner_keep, outer_send, inner_send = fence(
        (gram, outer_keep, inner_keep, outer_send, inner_send)
    )

    step = outer_keep.shape[0] // 2
    outer_got = swap(outer_send, "row", 1)
    zero, six = outer_keep[:step] + outer_got[:step], outer_keep[step:] + outer_got[step:]
    zero, six = fence((zero, six))
    six = swap(six, "row", 6)
    inner_got, far = fence((swap(inner_send, "row", 1), swap(gram, "row", bits[2])))
    gram = gram + far
    two, four = inner_keep[:step] + inner_got[:step], inner_keep[step:] + inner_got[step:]
    four, two = swap(four, "row", 4), swap(two, "row", 2)
    for bit in bits[3:]:
        gram = gram + swap(gram, "row", bit)
    six, four, two, far = fence((six, four, two, swap(gram, "col", 2)))
    state = gram + far
    zero = (zero + two) + (four + six)
    for bit in bits[3:]:
        zero = zero + swap(zero, "row", bit)
    zero, state = fence((zero, state))
    got = [swap(zero, "row", q) for q in (2, 4, 6, 1)]
    *got, state = fence((*got, factor(0, 6, state)))
    others, state = fence((jnp.concatenate(got[:3], 0), state))
    far, inverse = fence((swap(others, "row", 1), factor(6, 16, state)))
    projected, small = finish(own, inverse, [zero, others, got[3], far])

    across = [swap(small, "col", bit) for bit in (2, 3, 1)]
    *across, basis = fence((*across, dot(sketched, inverse, 1, 1)))
    small = (small + across[2]) + (across[0] + across[1])
    return (basis, projected, small / total_rows)


def solution(mesh):
    placed = (P("row", "col"), P("col", None))
    return jax.shard_map(
        per_device,
        mesh=mesh,
        in_specs=placed,
        out_specs=(P(("row", "col"), None), P(None, "col"), P()),
        check_vma=False,
    )
```
